32 devices in a mesh: parts: 2 (over y), node: 4 (over z), expert: 2 (over x), rep: 2 (over core).
Axes of the slice: x: 2, y: 2, z: 4, core: 2. Of those that a mesh axis runs over, the one named last changes fastest.
Arguments:
- token_values: bfloat16 [256, 5120], P(('parts', 'node', 'expert', 'rep')), parts along dimension 0, may hold values from -6 to 6
- block_scales: bfloat16 [256, 40], P(('parts', 'node', 'expert', 'rep')), parts along dimension 0, may hold values from 0.25 to 4
- expert_ids: int32 [256, 4], P(('parts', 'node', 'expert', 'rep')), parts along dimension 0, may hold values from 0 to 7, as said below
- gate_values: bfloat16 [256, 4], P(('parts', 'node', 'expert', 'rep')), parts along dimension 0, may hold values from 0.099609375 to 1
- gate_proj: bfloat16 [8, 5120, 1024], P(('node', 'rep'), None, 'expert'), may hold values from -0.078125 to 0.078125
- up_proj: bfloat16 [8, 5120, 1024], P(('node', 'rep'), None, 'expert'), may hold values from -0.078125 to 0.078125
- down_proj: bfloat16 [8, 1024, 5120], P(('node', 'rep'), None, 'expert'), may hold values from -0.1875 to 0.1875
Outputs:
- combined: bfloat16 [256, 5120], P(('parts', 'node', 'expert', 'rep')), parts along dimension 0
The draws below stay inside these ranges and needn't reach their ends.
There are 2 independent parts, one for each index of `parts`. The reference program is written for one: setup_inputs(seed, part) draws one part's arguments, and reference() takes and returns one part's arrays. A program takes and returns all parts, laid end to end along the dimension named above; an argument that names none is the same for every part. Nothing has to cross between parts.
Inputs may be any that keep to these rules, and one draw needn't show every extreme that they name: `expert_ids`: each token names 4 different experts lying in exactly 3 different node groups (expert e in group e // 2); in one of them it names both experts, in the others one. Among the 8 tokens of one device every node group is named by 6 - 1 to 6 tokens, and some group by exactly 6.
All inputs are finite; a program needn't handle non-finite values.
Results may differ from the reference program's by a relative error of at most 0.012.
Values may be sent and summed in bfloat16 or wider, within the bound.
A program may use at most 64 MiB of HBM per device.

```python
import math
import jax
import jax.numpy as jnp
from jax import lax

D = 5120
FF = 1024
TOPK = 4
LIMIT = 3
GROUP_EXP = 2
TOK_DEV = 8
EXPERTS = 8
CAP = 6
TOKENS = 128


def draw_expert_ids(key, part):
    key = jax.random.fold_in(key, 11)
    blocks = TOKENS // TOK_DEV
    groups = EXPERTS // GROUP_EXP
    order_key, double_key, side_key = jax.random.split(key, 3)
    shuffles = jax.vmap(lambda subkey: jax.random.permutation(subkey, groups))(jax.random.split(order_key, blocks))
    slot_index = (jnp.arange(TOK_DEV, dtype=jnp.int32)[:, None] * LIMIT + jnp.arange(LIMIT, dtype=jnp.int32)[None, :]) % groups
    chosen = shuffles[:, slot_index].astype(jnp.int32)
    double = jax.random.randint(double_key, (blocks, TOK_DEV, 1), 0, LIMIT)
    side_bits = jax.random.randint(side_key, (blocks, TOK_DEV, LIMIT), 0, GROUP_EXP)
    pick_double = jnp.take_along_axis(chosen, double, axis=2)[..., 0]
    other_one = jnp.take_along_axis(chosen, (double + 1) % LIMIT, axis=2)[..., 0]
    other_two = jnp.take_along_axis(chosen, (double + 2) % LIMIT, axis=2)[..., 0]
    side_one = jnp.take_along_axis(side_bits, (double + 1) % LIMIT, axis=2)[..., 0]
    side_two = jnp.take_along_axis(side_bits, (double + 2) % LIMIT, axis=2)[..., 0]
    picked_ids = jnp.stack([GROUP_EXP * pick_double, GROUP_EXP * pick_double + 1, GROUP_EXP * other_one + side_one, GROUP_EXP * other_two + side_two], axis=-1)
    return picked_ids.reshape(TOKENS, TOPK).astype(jnp.int32)


def levels(stream_key, dims, shards, least, high):
    def one(dim, blocks):
        heights = jax.random.uniform(jax.random.fold_in(jax.random.fold_in(stream_key, 6), dim), (blocks,), jnp.float32, least / len(shards), high / len(shards))
        return jnp.repeat(jnp.exp(heights), dims[dim] // blocks).reshape((-1,) + (1,) * (len(dims) - dim - 1))

    level = one(*shards[0])
    for cut in shards[1:]:
        level = level * one(*cut)
    return level


def noise(rng, dims, spread, limit, cuts=(), held_as=jnp.bfloat16):
    gain = levels(rng, dims, cuts, -0.22, 0.18) if cuts else 1.0
    drawn = jax.random.normal(rng, dims, jnp.float32) * spread * gain
    return jnp.minimum(jnp.maximum(drawn, -limit), limit).astype(held_as)


def setup_inputs(seed: int = 0, part: int = 0) -> dict:
    key_list = jax.random.split(jax.random.key(seed), 8)
    part_keys = jax.random.split(jax.random.fold_in(key_list[7], part), 8)
    token_values = noise(part_keys[0], (TOKENS, D), 1.0, 6.0, ((0, 16),))
    block_scales = jnp.clip(jnp.exp(math.log(4.0) - 2.7725887 * jax.random.uniform(part_keys[1], (TOKENS, D // 128), jnp.float32) ** levels(part_keys[1], (TOKENS, D // 128), ((0, 16),), -0.2, 0.2)), 0.25, 4.0).astype(jnp.bfloat16)
    expert_ids = draw_expert_ids(jax.random.fold_in(jax.random.fold_in(key_list[7], part), 71), part)
    gate_values = jnp.clip(0.099609375 + 0.9003906 * jax.random.uniform(part_keys[3], (TOKENS, TOPK), jnp.float32) ** levels(part_keys[3], (TOKENS, TOPK), ((0, 16),), -0.2, 0.2), 0.099609375, 1.0).astype(jnp.bfloat16)
    gate_proj = noise(key_list[4], (EXPERTS, D, FF), D ** -0.5, 0.078125, ((0, 8), (2, 2)))
    up_proj = noise(key_list[5], (EXPERTS, D, FF), D ** -0.5, 0.078125, ((0, 8), (2, 2)))
    down_proj = noise(key_list[6], (EXPERTS, FF, D), FF ** -0.5, 0.1875, ((0, 8), (2, 2)))
    return dict(token_values=token_values, block_scales=block_scales, expert_ids=expert_ids, gate_values=gate_values, gate_proj=gate_proj, up_proj=up_proj, down_proj=down_proj)


def dequantize(values, scales):
    count, width = values.shape
    blocks = values.astype(jnp.float32).reshape(count, width // 128, 128) * scales.astype(jnp.float32)[:, :, None]
    return blocks.reshape(count, width).astype(jnp.bfloat16)


def one_expert(operands):
    expert_rows, gate_matrix, up_matrix, down_matrix = operands
    gate_part = jnp.dot(expert_rows, gate_matrix, preferred_element_type=jnp.float32)
    up_part = jnp.dot(expert_rows, up_matrix, preferred_element_type=jnp.float32)
    hidden = (jax.nn.silu(gate_part) * up_part).astype(jnp.bfloat16)
    return jnp.dot(hidden, down_matrix, preferred_element_type=jnp.float32).astype(jnp.bfloat16)


def reference(token_values, block_scales, expert_ids, gate_values, gate_proj, up_proj, down_proj):
    dequantized = dequantize(token_values, block_scales)
    pair_experts = expert_ids.reshape(-1).astype(jnp.int32)
    owners = jnp.arange(TOKENS * TOPK, dtype=jnp.int32) // TOPK
    onehot = (pair_experts[:, None] == jnp.arange(EXPERTS, dtype=jnp.int32)[None, :]).astype(jnp.int32)
    before = jnp.cumsum(onehot, axis=0) - onehot
    position = jnp.sum(before * onehot, axis=1).astype(jnp.int32)
    capacity_rows = (TOKENS // TOK_DEV) * CAP
    buffer_index = (pair_experts * capacity_rows + position).astype(jnp.int32)
    slot_rows = jnp.zeros((EXPERTS * capacity_rows, D), dequantized.dtype)
    slot_rows = slot_rows.at[buffer_index].set(dequantized[owners])
    slot_rows = slot_rows.reshape(EXPERTS, capacity_rows, D)
    results = lax.map(one_expert, (slot_rows, gate_proj, up_proj, down_proj))
    picked = results.reshape(EXPERTS * capacity_rows, D)[buffer_index].reshape(TOKENS, TOPK, D)
    weighted = gate_values.astype(jnp.float32)[:, :, None] * picked.astype(jnp.float32)
    group_index = (expert_ids // GROUP_EXP).astype(jnp.int32)
    same_group = (group_index[:, :, None] == group_index[:, None, :]).astype(jnp.float32)
    group_total = jnp.einsum("tkj,tjd->tkd", same_group, weighted, precision=lax.Precision.HIGHEST).astype(jnp.bfloat16)
    earlier = jnp.arange(TOPK, dtype=jnp.int32)[None, :] < jnp.arange(TOPK, dtype=jnp.int32)[:, None]
    repeat = jnp.any((same_group > 0.5) & earlier[None, :, :], axis=2)
    first_seen = jnp.where(repeat, 0.0, 1.0).astype(jnp.float32)
    combined = jnp.sum(first_seen[:, :, None] * group_total.astype(jnp.float32), axis=1)
    return combined.astype(jnp.bfloat16)
```

```python
import functools

import jax
import jax.numpy as jnp
from jax import lax
from jax.experimental import pallas as pl
from jax.experimental.pallas import tpu as pltpu
from jax.sharding import PartitionSpec as P

LIMIT = 3
GROUP_EXP = 2


def dequantize(values, scales):
    lead_dims = values.shape[:-1]
    width = values.shape[-1]
    blocks = (
        values.astype(jnp.float32).reshape(lead_dims + (width // 128, 128))
        * scales.astype(jnp.float32)[..., None]
    )
    return blocks.reshape(values.shape).astype(jnp.bfloat16)


def per_device(token_values, block_scales, expert_ids, gate_values, gate_proj, up_proj, down_proj):
    groups = lax.axis_size("node")
    members = lax.axis_size("expert")
    tok_rows, width = token_values.shape
    block_count = block_scales.shape[1]
    capacity = (LIMIT * tok_rows + groups - 1) // groups
    gate_local = gate_proj[0]
    up_local = up_proj[0]
    down_local = down_proj[0]
    column_count = down_local.shape[1]
    group_index = expert_ids // GROUP_EXP
    side_index = expert_ids % GROUP_EXP
    group_hit = group_index[:, :, None] == jnp.arange(groups, dtype=jnp.int32)[None, None, :]
    in_group = jnp.any(group_hit, axis=1).astype(jnp.int32)
    ahead_count = jnp.cumsum(in_group, axis=0) - in_group
    slot_hit = (ahead_count[:, :, None] == jnp.arange(capacity, dtype=jnp.int32)[None, None, :]) & (
        in_group[:, :, None] > 0
    )
    assign = (
        jnp.transpose(slot_hit, (1, 2, 0)).reshape(groups * capacity, tok_rows).astype(jnp.bfloat16)
    )
    side_hit = (
        side_index[:, :, None] == jnp.arange(GROUP_EXP, dtype=jnp.int32)[None, None, :]
    ).astype(jnp.float32)
    pair_gates = jnp.einsum(
        "tkg,tks->tgs",
        group_hit.astype(jnp.float32),
        side_hit * gate_values.astype(jnp.float32)[:, :, None],
        precision=lax.Precision.HIGHEST,
    )
    send_gates = jnp.einsum(
        "tgc,tgs->gcs", slot_hit.astype(jnp.float32), pair_gates, precision=lax.Precision.HIGHEST
    ).astype(jnp.bfloat16)
    send_values = (
        jnp.dot(assign, token_values, preferred_element_type=jnp.float32)
        .astype(jnp.bfloat16)
        .reshape(groups, capacity, width)
    )
    send_scales = (
        jnp.dot(assign, block_scales, preferred_element_type=jnp.float32)
        .astype(jnp.bfloat16)
        .reshape(groups, capacity, block_count)
    )
    spread_values = jnp.broadcast_to(
        send_values[:, None], (groups, members, capacity, width)
    ).reshape(groups * members, capacity, width)
    spread_scales = jnp.broadcast_to(
        send_scales[:, None], (groups, members, capacity, block_count)
    ).reshape(groups * members, capacity, block_count)
    spread_gates = jnp.broadcast_to(
        send_gates[:, None], (groups, members, capacity, GROUP_EXP)
    ).reshape(groups * members, capacity, GROUP_EXP)
    got_values, got_scales, got_gates = (
        lax.all_to_all(spread_values, ("node", "expert"), split_axis=0, concat_axis=0, tiled=True),
        lax.all_to_all(spread_scales, ("node", "expert"), split_axis=0, concat_axis=0, tiled=True),
        lax.all_to_all(spread_gates, ("node", "expert"), split_axis=0, concat_axis=0, tiled=True),
    )
    side_values = got_values.reshape(groups, members, capacity, width)
    side_scales = got_scales.reshape(groups, members, capacity, block_count)
    side_gates = got_gates.reshape(groups, members, capacity, GROUP_EXP)
    pair_values, pair_scales, pair_slot_gates = (
        lax.all_gather(side_values[None], "rep", axis=0, tiled=True),
        lax.all_gather(side_scales[None], "rep", axis=0, tiled=True),
        lax.all_gather(side_gates[None], "rep", axis=0, tiled=True),
    )
    arrived = dequantize(pair_values, pair_scales).reshape(-1, width)
    gate_part = jnp.dot(arrived, gate_local, preferred_element_type=jnp.float32)
    up_part = jnp.dot(arrived, up_local, preferred_element_type=jnp.float32)
    hidden = (jax.nn.silu(gate_part) * up_part).astype(jnp.bfloat16)
    summed = jnp.dot(
        lax.all_gather(hidden, "expert", axis=1, tiled=True),
        down_local,
        preferred_element_type=jnp.float32,
    )
    expert_out = summed.astype(jnp.bfloat16)
    own_side = (jnp.arange(GROUP_EXP, dtype=jnp.int32) == lax.axis_index("rep")).astype(jnp.float32)
    gate_mine = jnp.sum(
        pair_slot_gates.reshape(-1, GROUP_EXP).astype(jnp.float32) * own_side[None, :], axis=1
    )
    gated_out = (gate_mine[:, None] * expert_out.astype(jnp.float32)).reshape(
        GROUP_EXP, -1, column_count
    )
    group_sum = lax.psum_scatter(
        gated_out.astype(jnp.bfloat16), "rep", scatter_dimension=0, tiled=True
    )
    outputs = group_sum.reshape(groups, members, capacity, column_count)
    flat_back = lax.all_to_all(
        outputs.reshape(groups * members, capacity, column_count),
        ("node", "expert"),
        split_axis=0,
        concat_axis=0,
        tiled=True,
    )
    returned = flat_back.reshape(groups, members, capacity, column_count)
    return_table = jnp.transpose(returned, (0, 2, 1, 3)).reshape(
        groups * capacity, members * column_count
    )
    combined = jnp.dot(assign.T, return_table, preferred_element_type=jnp.float32)
    return combined.astype(jnp.bfloat16)


NODES = 4
MESH = pl.DeviceIdType.MESH
PHASES = 2
TILES = 2


def fused_kernel(
    tok_ref, scale_ref, ids_ref, gate_ref, gate_hbm, up_hbm, down_hbm, out_ref,
    wg, wu, wd, slabs, rows, gates, acc_g, acc_u, hidden, acc_d,
    mate_out, mate_in, back_out, back_in, final, last_out, last_in,
    w_sem, recv_sem, z_sem, x_sem, m_sem, h_sem, r_sem, b_send, b_recv, f_sem,
):
    part = lax.axis_index("parts")
    n = lax.axis_index("node")
    e = lax.axis_index("expert")
    r = lax.axis_index("rep")
    width = tok_ref.shape[1]
    half = width // 2
    ff = wg.shape[1]
    step = half // PHASES

    weights = [
        pltpu.make_async_copy(gate_hbm.at[0], wg, w_sem.at[0]),
        pltpu.make_async_copy(up_hbm.at[0], wu, w_sem.at[1]),
        pltpu.make_async_copy(down_hbm.at[0], wd, w_sem.at[2]),
    ]
    for copy in weights:
        copy.start()

    near = n + 1 - 2 * (n % 2)
    peers = [near, (n + 2) % 4, 3 - n]
    z_devs = [(part, p, e, r) for p in peers]
    x_dev = (part, n, 1 - e, r)
    m_dev = (part, n, e, 1 - r)

    barrier = pltpu.get_barrier_semaphore()
    for dev in z_devs + [x_dev, m_dev]:
        pl.semaphore_signal(barrier, inc=1, device_id=dev, device_id_type=MESH)

    def slot(a, b, c):
        return (a * 2 + b) * 2 + c

    me = slot(n, e, r)
    scales = scale_ref[...].astype(jnp.float32)
    for j in range(half // 128):
        lo = tok_ref[:, j * 128:(j + 1) * 128].astype(jnp.float32) * scales[:, j:j + 1]
        k = j + half // 128
        hi = tok_ref[:, k * 128:(k + 1) * 128].astype(jnp.float32) * scales[:, k:k + 1]
        slabs[me, :, j * 128:(j + 1) * 128] = jnp.concatenate([lo, hi], axis=0).astype(jnp.bfloat16)
    lane = lax.broadcasted_iota(jnp.int32, (tok_ref.shape[0], 128), 1)
    table = jnp.zeros(lane.shape, jnp.float32)
    for k in range(ids_ref.shape[1]):
        table = table + jnp.where(
            ids_ref[:, k:k + 1] == lane, gate_ref[:, k:k + 1].astype(jnp.float32), 0.0
        )
    slabs[me, :, half:half + 128] = jnp.concatenate([table, table], axis=0).astype(jnp.bfloat16)

    pl.semaphore_wait(barrier, 5)

    def cols(c):
        stop = (c + 1) * step + (128 if c == PHASES - 1 else 0)
        return pl.ds(c * step, stop - c * step)

    def send(src, c, sem, dev):
        block = slabs.at[src, :, cols(c)]
        copy = pltpu.make_async_remote_copy(
            src_ref=block, dst_ref=block, send_sem=sem, recv_sem=recv_sem.at[src, c],
            device_id=dev, device_id_type=MESH,
        )
        copy.start()
        return copy

    def arrive(src, c):
        block = slabs.at[src, :, cols(c)]
        pltpu.make_async_remote_copy(
            src_ref=block, dst_ref=block, send_sem=m_sem.at[0, 0], recv_sem=recv_sem.at[src, c],
            device_id=m_dev, device_id_type=MESH,
        ).wait_recv()

    sent = []
    for c in range(PHASES):
        for i in (2, 1, 0):
            sent.append(send(me, c, z_sem.at[i, c], z_devs[i]))
        sent.append(send(me, c, x_sem.at[3, c], x_dev))
        sent.append(send(me, c, m_sem.at[3, c], m_dev))

    acc_g[...] = jnp.zeros_like(acc_g)
    acc_u[...] = jnp.zeros_like(acc_u)
    for c in range(PHASES):
        for i in range(3):
            src = slot(peers[i], e, r)
            arrive(src, c)
            sent.append(send(src, c, x_sem.at[i, c], x_dev))
            sent.append(send(src, c, m_sem.at[i, c], m_dev))
        for i, p in enumerate([n] + peers):
            src = slot(p, 1 - e, r)
            arrive(src, c)
            sent.append(send(src, c, m_sem.at[4 + i, c], m_dev))
        for p in [n] + peers:
            arrive(slot(p, e, 1 - r), c)
            arrive(slot(p, 1 - e, 1 - r), c)
        lo_cols = slice(c * step, (c + 1) * step)
        hi_cols = slice(half + c * step, half + (c + 1) * step)
        for rr in range(2):
            for nn in range(NODES):
                one = slabs[slot(nn, 0, rr), :, lo_cols].astype(jnp.float32)
                two = slabs[slot(nn, 1, rr), :, lo_cols].astype(jnp.float32)
                at = (rr * NODES + nn) * 16
                rows[at:at + 16, lo_cols] = jnp.concatenate([one[:8], two[:8]], axis=0).astype(jnp.bfloat16)
                rows[at:at + 16, hi_cols] = jnp.concatenate([one[8:], two[8:]], axis=0).astype(jnp.bfloat16)
        if c == 0:
            weights[0].wait()
            weights[1].wait()
        for span in (lo_cols, hi_cols):
            acc_g[...] += jnp.dot(rows[:, span], wg[span, :], preferred_element_type=jnp.float32)
            acc_u[...] += jnp.dot(rows[:, span], wu[span, :], preferred_element_type=jnp.float32)

    gate_v = acc_g[...]
    hidden[e] = ((gate_v / (1.0 + jnp.exp(-gate_v))) * acc_u[...]).astype(jnp.bfloat16)
    h_copy = pltpu.make_async_remote_copy(
        src_ref=hidden.at[e], dst_ref=hidden.at[e], send_sem=h_sem.at[0], recv_sem=h_sem.at[1],
        device_id=x_dev, device_id_type=MESH,
    )
    h_copy.start()

    mine = lax.broadcasted_iota(jnp.int32, (16, 128), 1) == n * 2 + r
    for rr in range(2):
        for nn in range(NODES):
            one = slabs[slot(nn, 0, rr), :, half:half + 128].astype(jnp.float32)
            two = slabs[slot(nn, 1, rr), :, half:half + 128].astype(jnp.float32)
            both = jnp.concatenate([one[:8], two[:8]], axis=0)
            at = (rr * NODES + nn) * 16
            picked = jnp.sum(jnp.where(mine, both, 0.0), axis=1, keepdims=True)
            gates[at:at + 16, :] = jnp.broadcast_to(picked, (16, 128))

    weights[2].wait()
    wide = wd.shape[1] // TILES
    own_ff = pl.ds(pl.multiple_of(e * ff, ff), ff)
    other_ff = pl.ds(pl.multiple_of((1 - e) * ff, ff), ff)
    for t in range(TILES):
        span = slice(t * wide, (t + 1) * wide)
        acc_d[:, span] = jnp.dot(hidden[e], wd[own_ff, span], preferred_element_type=jnp.float32)
    h_copy.wait()
    group_rows = NODES * 16
    own_rows = pl.ds(pl.multiple_of(r * group_rows, group_rows), group_rows)
    mate_rows = pl.ds(pl.multiple_of((1 - r) * group_rows, group_rows), group_rows)
    r_copies = []
    for t in range(TILES):
        span = slice(t * wide, (t + 1) * wide)
        acc_d[:, span] += jnp.dot(hidden[1 - e], wd[other_ff, span], preferred_element_type=jnp.float32)
        done = acc_d[mate_rows, span].astype(jnp.bfloat16).astype(jnp.float32)
        mate_out[:, span] = (done * gates[mate_rows, 0:1]).astype(jnp.bfloat16)
        copy = pltpu.make_async_remote_copy(
            src_ref=mate_out.at[:, span], dst_ref=mate_in.at[:, span],
            send_sem=r_sem.at[0, t], recv_sem=r_sem.at[1, t], device_id=m_dev, device_id_type=MESH,
        )
        copy.start()
        r_copies.append(copy)
    b_copies = []
    for t in range(TILES):
        span = slice(t * wide, (t + 1) * wide)
        r_copies[t].wait()
        done = acc_d[own_rows, span].astype(jnp.bfloat16).astype(jnp.float32)
        total = done * gates[own_rows, 0:1] + mate_in[:, span].astype(jnp.float32)
        back_out[:, span] = total.astype(jnp.bfloat16)
        for i in (2, 1, 0):
            from_rows = pl.ds(pl.multiple_of(peers[i] * 16, 16), 16)
            copy = pltpu.make_async_remote_copy(
                src_ref=back_out.at[from_rows, span], dst_ref=back_in.at[n, :, span],
                send_sem=b_send.at[i, t], recv_sem=b_recv.at[n, t],
                device_id=z_devs[i], device_id_type=MESH,
            )
            copy.start()
            b_copies.append(copy)
    for t in range(TILES):
        span = slice(t * wide, (t + 1) * wide)
        total = back_out[pl.ds(pl.multiple_of(n * 16, 16), 16), span].astype(jnp.float32)
        for i in range(3):
            pltpu.make_async_remote_copy(
                src_ref=back_in.at[peers[i], :, span], dst_ref=back_in.at[peers[i], :, span],
                send_sem=b_send.at[i, t], recv_sem=b_recv.at[peers[i], t],
                device_id=z_devs[i], device_id_type=MESH,
            ).wait_recv()
            total = total + back_in[peers[i], :, span].astype(jnp.float32)
        final[0, :, span] = total[:8]
        final[1, :, span] = total[8:]
    quarter = wd.shape[1] // 2
    last_out[...] = jnp.concatenate(
        [final[1 - e, :, :quarter], final[1 - e, :, quarter:]], axis=0
    ).astype(jnp.bfloat16)
    f_copy = pltpu.make_async_remote_copy(
        src_ref=last_out, dst_ref=last_in, send_sem=f_sem.at[0], recv_sem=f_sem.at[1],
        device_id=x_dev, device_id_type=MESH,
    )
    f_copy.start()
    out_ref[:, pl.ds(pl.multiple_of(e * half, half), half)] = final[e].astype(jnp.bfloat16)
    f_copy.wait()
    other = last_in[...].astype(jnp.float32)
    base = (1 - e) * half
    out_ref[:, pl.ds(pl.multiple_of(base, quarter), quarter)] = other[:8].astype(jnp.bfloat16)
    out_ref[:, pl.ds(pl.multiple_of(base + quarter, quarter), quarter)] = other[8:].astype(jnp.bfloat16)
    for copy in sent + b_copies:
        copy.wait_send()


def fused_device(token_values, block_scales, expert_ids, gate_values, gate_proj, up_proj, down_proj):
    tok_rows, width = token_values.shape
    half = width // 2
    ff = gate_proj.shape[2]
    total_rows = NODES * 4 * tok_rows
    column_count = down_proj.shape[2]
    vmem = pl.BlockSpec(memory_space=pltpu.VMEM)
    hbm = pl.BlockSpec(memory_space=pl.ANY)
    bf16, f32 = jnp.bfloat16, jnp.float32
    dma = pltpu.SemaphoreType.DMA
    return pl.pallas_call(
        fused_kernel,
        out_shape=jax.ShapeDtypeStruct((tok_rows, width), bf16),
        in_specs=[vmem] * 4 + [hbm] * 3,
        out_specs=vmem,
        scratch_shapes=[
            pltpu.VMEM((width, ff), bf16),
            pltpu.VMEM((width, ff), bf16),
            pltpu.VMEM((2 * ff, column_count), bf16),
            pltpu.VMEM((NODES * 4, 2 * tok_rows, half + 128), bf16),
            pltpu.VMEM((total_rows, width), bf16),
            pltpu.VMEM((total_rows, 128), f32),
            pltpu.VMEM((total_rows, ff), f32),
            pltpu.VMEM((total_rows, ff), f32),
            pltpu.VMEM((2, total_rows, ff), bf16),
            pltpu.VMEM((total_rows, column_count), f32),
            pltpu.VMEM((total_rows // 2, column_count), bf16),
            pltpu.VMEM((total_rows // 2, column_count), bf16),
            pltpu.VMEM((total_rows // 2, column_count), bf16),
            pltpu.VMEM((NODES, 2 * tok_rows, column_count), bf16),
            pltpu.VMEM((2, tok_rows, column_count), f32),
            pltpu.VMEM((2 * tok_rows, column_count // 2), bf16),
            pltpu.VMEM((2 * tok_rows, column_count // 2), bf16),
            dma((3,)),
            dma((NODES * 4, PHASES)),
            dma((3, PHASES)),
            dma((4, PHASES)),
            dma((8, PHASES)),
            dma((2,)),
            dma((2, TILES)),
            dma((3, TILES)),
            dma((NODES, TILES)),
            dma((2,)),
        ],
        compiler_params=pltpu.CompilerParams(
            collective_id=1, has_side_effects=True, vmem_limit_bytes=52 * 1024 * 1024
        ),
        cost_estimate=pl.CostEstimate(
            flops=2 * total_rows * width * ff * 3, bytes_accessed=6 * width * ff, transcendentals=0
        ),
    )(token_values, block_scales, expert_ids, gate_values, gate_proj, up_proj, down_proj)


def solution(mesh):
    sizes = mesh.shape
    fits = (sizes["node"], sizes["expert"], sizes["rep"]) == (4, 2, 2)
    return jax.shard_map(
        fused_device if fits else per_device,
        mesh=mesh,
        in_specs=(
            P(("parts", "node", "expert", "rep"), None),
            P(("parts", "node", "expert", "rep"), None),
            P(("parts", "node", "expert", "rep"), None),
            P(("parts", "node", "expert", "rep"), None),
            P(("node", "rep"), None, "expert"),
            P(("node", "rep"), None, "expert"),
            P(("node", "rep"), None, "expert"),
        ),
        out_specs=P(("parts", "node", "expert", "rep"), None),
        check_vma=False,
    )
```

```python
import functools

import jax
import jax.numpy as jnp
from jax import lax
from jax.experimental import pallas as pl
from jax.experimental.pallas import tpu as pltpu
from jax.sharding import PartitionSpec as P

LIMIT = 3
GROUP_EXP = 2


def dequantize(values, scales):
    lead_dims = values.shape[:-1]
    width = values.shape[-1]
    blocks = (
        values.astype(jnp.float32).reshape(lead_dims + (width // 128, 128))
        * scales.astype(jnp.float32)[..., None]
    )
    return blocks.reshape(values.shape).astype(jnp.bfloat16)


def per_device(token_values, block_scales, expert_ids, gate_values, gate_proj, up_proj, down_proj):
    groups = lax.axis_size("node")
    members = lax.axis_size("expert")
    tok_rows, width = token_values.shape
    block_count = block_scales.shape[1]
    capacity = (LIMIT * tok_rows + groups - 1) // groups
    gate_local = gate_proj[0]
    up_local = up_proj[0]
    down_local = down_proj[0]
    column_count = down_local.shape[1]
    group_index = expert_ids // GROUP_EXP
    side_index = expert_ids % GROUP_EXP
    group_hit = group_index[:, :, None] == jnp.arange(groups, dtype=jnp.int32)[None, None, :]
    in_group = jnp.any(group_hit, axis=1).astype(jnp.int32)
    ahead_count = jnp.cumsum(in_group, axis=0) - in_group
    slot_hit = (ahead_count[:, :, None] == jnp.arange(capacity, dtype=jnp.int32)[None, None, :]) & (
        in_group[:, :, None] > 0
    )
    assign = (
        jnp.transpose(slot_hit, (1, 2, 0)).reshape(groups * capacity, tok_rows).astype(jnp.bfloat16)
    )
    side_hit = (
        side_index[:, :, None] == jnp.arange(GROUP_EXP, dtype=jnp.int32)[None, None, :]
    ).astype(jnp.float32)
    pair_gates = jnp.einsum(
        "tkg,tks->tgs",
        group_hit.astype(jnp.float32),
        side_hit * gate_values.astype(jnp.float32)[:, :, None],
        precision=lax.Precision.HIGHEST,
    )
    send_gates = jnp.einsum(
        "tgc,tgs->gcs", slot_hit.astype(jnp.float32), pair_gates, precision=lax.Precision.HIGHEST
    ).astype(jnp.bfloat16)
    send_values = (
        jnp.dot(assign, token_values, preferred_element_type=jnp.float32)
        .astype(jnp.bfloat16)
        .reshape(groups, capacity, width)
    )
    send_scales = (
        jnp.dot(assign, block_scales, preferred_element_type=jnp.float32)
        .astype(jnp.bfloat16)
        .reshape(groups, capacity, block_count)
    )
    spread_values = jnp.broadcast_to(
        send_values[:, None], (groups, members, capacity, width)
    ).reshape(groups * members, capacity, width)
    spread_scales = jnp.broadcast_to(
        send_scales[:, None], (groups, members, capacity, block_count)
    ).reshape(groups * members, capacity, block_count)
    spread_gates = jnp.broadcast_to(
        send_gates[:, None], (groups, members, capacity, GROUP_EXP)
    ).reshape(groups * members, capacity, GROUP_EXP)
    got_values, got_scales, got_gates = (
        lax.all_to_all(spread_values, ("node", "expert"), split_axis=0, concat_axis=0, tiled=True),
        lax.all_to_all(spread_scales, ("node", "expert"), split_axis=0, concat_axis=0, tiled=True),
        lax.all_to_all(spread_gates, ("node", "expert"), split_axis=0, concat_axis=0, tiled=True),
    )
    side_values = got_values.reshape(groups, members, capacity, width)
    side_scales = got_scales.reshape(groups, members, capacity, block_count)
    side_gates = got_gates.reshape(groups, members, capacity, GROUP_EXP)
    pair_values, pair_scales, pair_slot_gates = (
        lax.all_gather(side_values[None], "rep", axis=0, tiled=True),
        lax.all_gather(side_scales[None], "rep", axis=0, tiled=True),
        lax.all_gather(side_gates[None], "rep", axis=0, tiled=True),
    )
    arrived = dequantize(pair_values, pair_scales).reshape(-1, width)
    gate_part = jnp.dot(arrived, gate_local, preferred_element_type=jnp.float32)
    up_part = jnp.dot(arrived, up_local, preferred_element_type=jnp.float32)
    hidden = (jax.nn.silu(gate_part) * up_part).astype(jnp.bfloat16)
    summed = jnp.dot(
        lax.all_gather(hidden, "expert", axis=1, tiled=True),
        down_local,
        preferred_element_type=jnp.float32,
    )
    expert_out = summed.astype(jnp.bfloat16)
    own_side = (jnp.arange(GROUP_EXP, dtype=jnp.int32) == lax.axis_index("rep")).astype(jnp.float32)
    gate_mine = jnp.sum(
        pair_slot_gates.reshape(-1, GROUP_EXP).astype(jnp.float32) * own_side[None, :], axis=1
    )
    gated_out = (gate_mine[:, None] * expert_out.astype(jnp.float32)).reshape(
        GROUP_EXP, -1, column_count
    )
    group_sum = lax.psum_scatter(
        gated_out.astype(jnp.bfloat16), "rep", scatter_dimension=0, tiled=True
    )
    outputs = group_sum.reshape(groups, members, capacity, column_count)
    flat_back = lax.all_to_all(
        outputs.reshape(groups * members, capacity, column_count),
        ("node", "expert"),
        split_axis=0,
        concat_axis=0,
        tiled=True,
    )
    returned = flat_back.reshape(groups, members, capacity, column_count)
    return_table = jnp.transpose(returned, (0, 2, 1, 3)).reshape(
        groups * capacity, members * column_count
    )
    combined = jnp.dot(assign.T, return_table, preferred_element_type=jnp.float32)
    return combined.astype(jnp.bfloat16)


NODES = 4
SLOTS = 8
USED = 6
BLOCKS = 3
MESH = pl.DeviceIdType.MESH


def by_slots(value):
    return value.reshape(value.shape[0] // SLOTS, SLOTS, value.shape[1])


def pack(value):
    wide = value.shape[1] // 4
    spare = by_slots(value[:, 3 * wide:])
    row = lax.broadcasted_iota(jnp.int32, spare.shape, 1)
    blocks = []
    for b in range(BLOCKS):
        moved = pltpu.roll(spare, USED - 2 * b, 1)
        kept = by_slots(value[:, b * wide:(b + 1) * wide])
        blocks.append(jnp.where(row >= USED, moved, kept).reshape(value.shape[0], wide))
    return blocks


def unpack_spare(blocks):
    threes = [by_slots(block) for block in blocks]
    row = lax.broadcasted_iota(jnp.int32, threes[0].shape, 1)
    moved = [pltpu.roll(threes[b], SLOTS - USED + 2 * b, 1) for b in range(BLOCKS)]
    spare = jnp.where(row < 2, moved[0], jnp.where(row < 4, moved[1], moved[2]))
    return spare.reshape(blocks[0].shape)


def fused_kernel(
    tok_hbm, scale_hbm, ids_hbm, gate_hbm, gate_w_hbm, up_hbm, down_hbm, out_ref,
    tok_ref, scale_ref, ids_ref, gate_ref,
    wg, wu, wd, zout, slabs, rows, gates, acc_g, acc_u, hid_out, hid_in, hidden, acc_d,
    mate_out, mate_in, sums, back_out, back_in, final, last_out, last_in, place, place_in,
    w_sem, recv_sem, z_sem, x_sem, m_sem, h_sem, r_sem, b_send, b_recv, f_sem, p_sem,
):
    part = lax.axis_index("parts")
    n = lax.axis_index("node")
    e = lax.axis_index("expert")
    r = lax.axis_index("rep")
    width = tok_ref.shape[1]
    half = width // 2
    ff = wg.shape[1]
    step = half // 4
    packed = BLOCKS * step
    bf16, f32 = jnp.bfloat16, jnp.float32

    small = [
        pltpu.make_async_copy(src, dst, w_sem.at[3 + i])
        for i, (src, dst) in enumerate(
            [(tok_hbm, tok_ref), (scale_hbm, scale_ref), (ids_hbm, ids_ref), (gate_hbm, gate_ref)]
        )
    ]
    weights = [
        pltpu.make_async_copy(gate_w_hbm.at[0], wg, w_sem.at[0]),
        pltpu.make_async_copy(up_hbm.at[0], wu, w_sem.at[1]),
        pltpu.make_async_copy(down_hbm.at[0], wd, w_sem.at[2]),
    ]
    for copy in small + weights:
        copy.start()

    near = n + 1 - 2 * (n % 2)
    peers = [(n + 2) % 4, 3 - n, near]
    z_devs = [(part, p, e, r) for p in peers]
    x_dev = (part, n, 1 - e, r)
    m_dev = (part, n, e, 1 - r)

    barrier = pltpu.get_barrier_semaphore()
    for dev in z_devs + [x_dev, m_dev]:
        pl.semaphore_signal(barrier, inc=1, device_id=dev, device_id_type=MESH)

    def slot(a, b, c):
        return (a * 2 + b) * 2 + c

    me = slot(n, e, r)
    for copy in small:
        copy.wait()
    lane = lax.broadcasted_iota(jnp.int32, (SLOTS, 128), 1)
    table = jnp.zeros(lane.shape, f32)
    hit = jnp.zeros(lane.shape, f32)
    for k in range(ids_ref.shape[1]):
        chosen = ids_ref[:, k:k + 1]
        table = table + jnp.where(chosen == lane, gate_ref[:, k:k + 1].astype(f32), 0.0)
        hit = jnp.maximum(hit, jnp.where((chosen >> 1) == (lane >> 3), 1.0, 0.0))
    row = lax.broadcasted_iota(jnp.int32, lane.shape, 0)
    ahead = jnp.zeros(lane.shape, f32)
    for k in range(1, SLOTS):
        ahead = ahead + jnp.where(row >= k, pltpu.roll(hit, k, 0), 0.0)
    place[...] = jnp.where(ahead == (lane & 7).astype(f32), hit, 0.0)
    assign = place[...].T[:NODES * SLOTS].astype(bf16)
    scales = scale_ref[...].astype(f32)
    count = half // 128
    for h in range(2):
        pieces = [
            tok_ref[:, j * 128:(j + 1) * 128].astype(f32) * scales[:, j:j + 1]
            for j in range(h * count, (h + 1) * count)
        ]
        values = jnp.concatenate(pieces, axis=1).astype(bf16)
        placed = jnp.dot(assign, values, preferred_element_type=f32)
        for b, block in enumerate(pack(placed)):
            rows[h * 32:(h + 1) * 32, b * step:(b + 1) * step] = block.astype(bf16)
    slot_gates = jnp.dot(assign, table.astype(bf16), preferred_element_type=f32)
    for g in range(NODES):
        at = g * SLOTS
        for b in range(BLOCKS):
            span = slice(b * step, (b + 1) * step)
            lo = rows[0:32, span].astype(f32)[at:at + SLOTS]
            hi = rows[32:64, span].astype(f32)[at:at + SLOTS]
            zout[g, :, span] = jnp.concatenate([lo, hi], axis=0).astype(bf16)
        some = slot_gates[at:at + SLOTS]
        zout[g, :, packed:packed + 128] = jnp.concatenate([some, some], axis=0).astype(bf16)

    pl.semaphore_wait(barrier, 5)

    def cols(c):
        return pl.ds(c * step, step + (128 if c == BLOCKS - 1 else 0))

    def send(src_ref, src, c, sem, dev):
        copy = pltpu.make_async_remote_copy(
            src_ref=src_ref.at[:, cols(c)], dst_ref=slabs.at[src, :, cols(c)],
            send_sem=sem, recv_sem=recv_sem.at[src, c], device_id=dev, device_id_type=MESH,
        )
        copy.start()
        return copy

    def arrive(src, c):
        block = slabs.at[src, :, cols(c)]
        pltpu.make_async_remote_copy(
            src_ref=block, dst_ref=block, send_sem=m_sem.at[0, 0], recv_sem=recv_sem.at[src, c],
            device_id=m_dev, device_id_type=MESH,
        ).wait_recv()

    p_copy = pltpu.make_async_remote_copy(
        src_ref=place, dst_ref=place_in, send_sem=p_sem.at[0], recv_sem=p_sem.at[1],
        device_id=x_dev, device_id_type=MESH,
    )
    sent = []
    for c in range(BLOCKS):
        for i in range(3):
            sent.append(send(zout.at[peers[i]], me, c, z_sem.at[i, c], z_devs[i]))
        sent.append(send(zout.at[n], me, c, x_sem.at[3, c], x_dev))
        sent.append(send(zout.at[n], me, c, m_sem.at[3, c], m_dev))
    p_copy.start()
    slabs[me] = zout[n]

    def pass_z(c):
        for i in range(3):
            src = slot(peers[i], e, r)
            arrive(src, c)
            sent.append(send(slabs.at[src], src, c, x_sem.at[i, c], x_dev))
            sent.append(send(slabs.at[src], src, c, m_sem.at[i, c], m_dev))

    def pass_x(c):
        for i, p in enumerate([n] + peers):
            src = slot(p, 1 - e, r)
            arrive(src, c)
            sent.append(send(slabs.at[src], src, c, m_sem.at[4 + i, c], m_dev))

    pairs = [(rr * NODES + nn, slot(nn, 0, rr), slot(nn, 1, rr)) for rr in range(2) for nn in range(NODES)]
    acc_g[...] = jnp.zeros_like(acc_g)
    acc_u[...] = jnp.zeros_like(acc_u)

    def project(first):
        span = slice(first, first + step)
        acc_g[...] += jnp.dot(rows[:, span], wg[span, :], preferred_element_type=f32)
        acc_u[...] += jnp.dot(rows[:, span], wu[span, :], preferred_element_type=f32)

    pass_z(0)
    for c in range(BLOCKS):
        pass_x(c)
        if c + 1 < BLOCKS:
            pass_z(c + 1)
        for p in [n] + peers:
            arrive(slot(p, e, 1 - r), c)
            arrive(slot(p, 1 - e, 1 - r), c)
        span = slice(c * step, (c + 1) * step)
        for at, one, two in pairs:
            left = slabs[one, :, span].astype(f32)
            right = slabs[two, :, span].astype(f32)
            for h in range(2):
                cut = slice(h * SLOTS, (h + 1) * SLOTS)
                rows[at * 16:at * 16 + 16, h * half + c * step:h * half + (c + 1) * step] = (
                    jnp.concatenate([left[cut], right[cut]], axis=0).astype(bf16)
                )
        if c == 0:
            weights[0].wait()
            weights[1].wait()
        for h in range(2):
            project(h * half + c * step)
    for h in range(2):
        base = h * half
        for at in range(8):
            blocks = [
                rows[at * 16:at * 16 + 16, base + b * step:base + (b + 1) * step].astype(f32)
                for b in range(BLOCKS)
            ]
            rows[at * 16:at * 16 + 16, base + packed:base + half] = unpack_spare(blocks).astype(bf16)
        project(base + packed)

    gate_v = acc_g[...]
    active = (gate_v / (1.0 + jnp.exp(-gate_v))) * acc_u[...]
    piece = ff // 4
    for b, block in enumerate(pack(active)):
        hid_out[:, b * piece:(b + 1) * piece] = block.astype(bf16)
    h_copy = pltpu.make_async_remote_copy(
        src_ref=hid_out, dst_ref=hid_in, send_sem=h_sem.at[0], recv_sem=h_sem.at[1],
        device_id=x_dev, device_id_type=MESH,
    )
    h_copy.start()
    hidden[...] = active.astype(bf16)

    mine = lax.broadcasted_iota(jnp.int32, (16, 128), 1) == n * 2 + r
    for at, one, two in pairs:
        left = slabs[one, :, packed:packed + 128].astype(f32)
        right = slabs[two, :, packed:packed + 128].astype(f32)
        both = jnp.concatenate([left[:SLOTS], right[:SLOTS]], axis=0)
        picked = jnp.sum(jnp.where(mine, both, 0.0), axis=1, keepdims=True)
        gates[at * 16:at * 16 + 16, :] = jnp.broadcast_to(picked, (16, 128))

    weights[2].wait()
    tiles = [slice(t * step, (t + 1) * step) for t in (3, 0, 1, 2)]
    own_ff = pl.ds(pl.multiple_of(e * ff, ff), ff)
    other_ff = pl.ds(pl.multiple_of((1 - e) * ff, ff), ff)
    for span in tiles:
        acc_d[:, span] = jnp.dot(hidden[...], wd[own_ff, span], preferred_element_type=f32)
    h_copy.wait()
    blocks = [hid_in[:, b * piece:(b + 1) * piece].astype(f32) for b in range(BLOCKS)]
    hidden[:, :BLOCKS * piece] = hid_in[...]
    hidden[:, BLOCKS * piece:] = unpack_spare(blocks).astype(bf16)
    group_rows = NODES * 16
    own_rows = pl.ds(pl.multiple_of(r * group_rows, group_rows), group_rows)
    mate_rows = pl.ds(pl.multiple_of((1 - r) * group_rows, group_rows), group_rows)
    r_copies = []
    b_copies = []

    def give(t):
        span = tiles[t]
        acc_d[:, span] += jnp.dot(hidden[...], wd[other_ff, span], preferred_element_type=f32)
        done = acc_d[mate_rows, span].astype(bf16).astype(f32)
        mate_out[:, span] = (done * gates[mate_rows, 0:1]).astype(bf16)
        copy = pltpu.make_async_remote_copy(
            src_ref=mate_out.at[:, span], dst_ref=mate_in.at[:, span],
            send_sem=r_sem.at[0, t], recv_sem=r_sem.at[1, t], device_id=m_dev, device_id_type=MESH,
        )
        copy.start()
        r_copies.append(copy)

    def take(t):
        span = tiles[t]
        r_copies[t].wait()
        done = acc_d[own_rows, span].astype(bf16).astype(f32)
        total = done * gates[own_rows, 0:1] + mate_in[:, span].astype(f32)
        if t == 0:
            sums[...] = total
            return
        b = t - 1
        spare = pltpu.roll(by_slots(sums[...]), USED - 2 * b, 1)
        slots = lax.broadcasted_iota(jnp.int32, spare.shape, 1)
        mixed = jnp.where(slots >= USED, spare, by_slots(total)).reshape(total.shape)
        back_out[:, span] = mixed.astype(bf16)
        for i in range(3):
            from_rows = pl.ds(pl.multiple_of(peers[i] * 16, 16), 16)
            copy = pltpu.make_async_remote_copy(
                src_ref=back_out.at[from_rows, span], dst_ref=back_in.at[n, :, span],
                send_sem=b_send.at[i, b], recv_sem=b_recv.at[n, b],
                device_id=z_devs[i], device_id_type=MESH,
            )
            copy.start()
            b_copies.append(copy)

    give(0)
    give(1)
    take(0)
    give(2)
    take(1)
    give(3)
    take(2)
    take(3)
    back_in[n] = back_out[pl.ds(pl.multiple_of(n * 16, 16), 16), :]
    p_copy.wait()
    own_lanes = place[...].astype(bf16)[:, :NODES * SLOTS]
    other_lanes = place_in[...].astype(bf16)[:, :NODES * SLOTS]
    for b in range(BLOCKS):
        span = slice(b * step, (b + 1) * step)
        for i in range(3):
            block = back_in.at[peers[i], :, span]
            pltpu.make_async_remote_copy(
                src_ref=block, dst_ref=block,
                send_sem=b_send.at[i, b], recv_sem=b_recv.at[peers[i], b],
                device_id=z_devs[i], device_id_type=MESH,
            ).wait_recv()
    for b in range(BLOCKS):
        span = slice(b * step, (b + 1) * step)
        parts = [back_in[g, :, span].astype(f32) for g in range(NODES)]
        for h in range(2):
            final[h, :, span] = jnp.concatenate(
                [value[h * SLOTS:(h + 1) * SLOTS] for value in parts], axis=0
            )
    for h in range(2):
        final[h, :, packed:] = unpack_spare(
            [final[h, :, b * step:(b + 1) * step] for b in range(BLOCKS)]
        )
    theirs = jnp.dot(other_lanes, final[1 - e].astype(bf16), preferred_element_type=f32)
    quarter = half // 2
    last_out[...] = jnp.concatenate([theirs[:, :quarter], theirs[:, quarter:]], axis=0).astype(bf16)
    f_copy = pltpu.make_async_remote_copy(
        src_ref=last_out, dst_ref=last_in, send_sem=f_sem.at[0], recv_sem=f_sem.at[1],
        device_id=x_dev, device_id_type=MESH,
    )
    f_copy.start()
    ours = jnp.dot(own_lanes, final[e].astype(bf16), preferred_element_type=f32)
    out_ref[:, pl.ds(pl.multiple_of(e * half, half), half)] = ours.astype(bf16)
    f_copy.wait()
    other = last_in[...].astype(f32)
    base = (1 - e) * half
    out_ref[:, pl.ds(pl.multiple_of(base, quarter), quarter)] = other[:SLOTS].astype(bf16)
    out_ref[:, pl.ds(pl.multiple_of(base + quarter, quarter), quarter)] = other[SLOTS:].astype(bf16)
    for copy in sent + b_copies:
        copy.wait_send()


def fused_device(token_values, block_scales, expert_ids, gate_values, gate_proj, up_proj, down_proj):
    tok_rows, width = token_values.shape
    packed = width // 8 * BLOCKS
    ff = gate_proj.shape[2]
    total_rows = NODES * 4 * tok_rows
    column_count = down_proj.shape[2]
    vmem = pl.BlockSpec(memory_space=pltpu.VMEM)
    hbm = pl.BlockSpec(memory_space=pl.ANY)
    bf16, f32 = jnp.bfloat16, jnp.float32
    dma = pltpu.SemaphoreType.DMA
    return pl.pallas_call(
        fused_kernel,
        out_shape=jax.ShapeDtypeStruct((tok_rows, width), bf16),
        in_specs=[hbm] * 7,
        out_specs=vmem,
        scratch_shapes=[
            pltpu.VMEM(token_values.shape, bf16),
            pltpu.VMEM(block_scales.shape, bf16),
            pltpu.VMEM(expert_ids.shape, jnp.int32),
            pltpu.VMEM(gate_values.shape, bf16),
            pltpu.VMEM((width, ff), bf16),
            pltpu.VMEM((width, ff), bf16),
            pltpu.VMEM((2 * ff, column_count), bf16),
            pltpu.VMEM((NODES, 16, packed + 128), bf16),
            pltpu.VMEM((NODES * 4, 16, packed + 128), bf16),
            pltpu.VMEM((total_rows, width), bf16),
            pltpu.VMEM((total_rows, 128), f32),
            pltpu.VMEM((total_rows, ff), f32),
            pltpu.VMEM((total_rows, ff), f32),
            pltpu.VMEM((total_rows, ff // 4 * BLOCKS), bf16),
            pltpu.VMEM((total_rows, ff // 4 * BLOCKS), bf16),
            pltpu.VMEM((total_rows, ff), bf16),
            pltpu.VMEM((total_rows, column_count), f32),
            pltpu.VMEM((total_rows // 2, column_count), bf16),
            pltpu.VMEM((total_rows // 2, column_count), bf16),
            pltpu.VMEM((total_rows // 2, column_count // 4), f32),
            pltpu.VMEM((total_rows // 2, packed), bf16),
            pltpu.VMEM((NODES, 16, packed), bf16),
            pltpu.VMEM((2, NODES * SLOTS, column_count), f32),
            pltpu.VMEM((16, column_count // 2), bf16),
            pltpu.VMEM((16, column_count // 2), bf16),
            pltpu.VMEM((SLOTS, 128), f32),
            pltpu.VMEM((SLOTS, 128), f32),
            dma((7,)),
            dma((NODES * 4, BLOCKS)),
            dma((3, BLOCKS)),
            dma((4, BLOCKS)),
            dma((8, BLOCKS)),
            dma((2,)),
            dma((2, 4)),
            dma((3, BLOCKS)),
            dma((NODES, BLOCKS)),
            dma((2,)),
            dma((2,)),
        ],
        compiler_params=pltpu.CompilerParams(
            collective_id=1, has_side_effects=True, vmem_limit_bytes=52 * 1024 * 1024
        ),
        cost_estimate=pl.CostEstimate(
            flops=2 * total_rows * width * ff * 3, bytes_accessed=6 * width * ff, transcendentals=0
        ),
    )(token_values, block_scales, expert_ids, gate_values, gate_proj, up_proj, down_proj)


def solution(mesh):
    sizes = mesh.shape
    fits = (sizes["node"], sizes["expert"], sizes["rep"]) == (4, 2, 2)
    return jax.shard_map(
        fused_device if fits else per_device,
        mesh=mesh,
        in_specs=(
            P(("parts", "node", "expert", "rep"), None),
            P(("parts", "node", "expert", "rep"), None),
            P(("parts", "node", "expert", "rep"), None),
            P(("parts", "node", "expert", "rep"), None),
            P(("node", "rep"), None, "expert"),
            P(("node", "rep"), None, "expert"),
            P(("node", "rep"), None, "expert"),
        ),
        out_specs=P(("parts", "node", "expert", "rep"), None),
        check_vma=False,
    )
```

```python
import functools

import jax
import jax.numpy as jnp
from jax import lax
from jax.experimental import pallas as pl
from jax.experimental.pallas import tpu as pltpu
from jax.sharding import PartitionSpec as P

LIMIT = 3
GROUP_EXP = 2


def dequantize(values, scales):
    lead_dims = values.shape[:-1]
    width = values.shape[-1]
    blocks = (
        values.astype(jnp.float32).reshape(lead_dims + (width // 128, 128))
        * scales.astype(jnp.float32)[..., None]
    )
    return blocks.reshape(values.shape).astype(jnp.bfloat16)


def per_device(token_values, block_scales, expert_ids, gate_values, gate_proj, up_proj, down_proj):
    groups = lax.axis_size("node")
    members = lax.axis_size("expert")
    tok_rows, width = token_values.shape
    block_count = block_scales.shape[1]
    capacity = (LIMIT * tok_rows + groups - 1) // groups
    gate_local = gate_proj[0]
    up_local = up_proj[0]
    down_local = down_proj[0]
    column_count = down_local.shape[1]
    group_index = expert_ids // GROUP_EXP
    side_index = expert_ids % GROUP_EXP
    group_hit = group_index[:, :, None] == jnp.arange(groups, dtype=jnp.int32)[None, None, :]
    in_group = jnp.any(group_hit, axis=1).astype(jnp.int32)
    ahead_count = jnp.cumsum(in_group, axis=0) - in_group
    slot_hit = (ahead_count[:, :, None] == jnp.arange(capacity, dtype=jnp.int32)[None, None, :]) & (
        in_group[:, :, None] > 0
    )
    assign = (
        jnp.transpose(slot_hit, (1, 2, 0)).reshape(groups * capacity, tok_rows).astype(jnp.bfloat16)
    )
    side_hit = (
        side_index[:, :, None] == jnp.arange(GROUP_EXP, dtype=jnp.int32)[None, None, :]
    ).astype(jnp.float32)
    pair_gates = jnp.einsum(
        "tkg,tks->tgs",
        group_hit.astype(jnp.float32),
        side_hit * gate_values.astype(jnp.float32)[:, :, None],
        precision=lax.Precision.HIGHEST,
    )
    send_gates = jnp.einsum(
        "tgc,tgs->gcs", slot_hit.astype(jnp.float32), pair_gates, precision=lax.Precision.HIGHEST
    ).astype(jnp.bfloat16)
    send_values = (
        jnp.dot(assign, token_values, preferred_element_type=jnp.float32)
        .astype(jnp.bfloat16)
        .reshape(groups, capacity, width)
    )
    send_scales = (
        jnp.dot(assign, block_scales, preferred_element_type=jnp.float32)
        .astype(jnp.bfloat16)
        .reshape(groups, capacity, block_count)
    )
    spread_values = jnp.broadcast_to(
        send_values[:, None], (groups, members, capacity, width)
    ).reshape(groups * members, capacity, width)
    spread_scales = jnp.broadcast_to(
        send_scales[:, None], (groups, members, capacity, block_count)
    ).reshape(groups * members, capacity, block_count)
    spread_gates = jnp.broadcast_to(
        send_gates[:, None], (groups, members, capacity, GROUP_EXP)
    ).reshape(groups * members, capacity, GROUP_EXP)
    got_values, got_scales, got_gates = (
        lax.all_to_all(spread_values, ("node", "expert"), split_axis=0, concat_axis=0, tiled=True),
        lax.all_to_all(spread_scales, ("node", "expert"), split_axis=0, concat_axis=0, tiled=True),
        lax.all_to_all(spread_gates, ("node", "expert"), split_axis=0, concat_axis=0, tiled=True),
    )
    side_values = got_values.reshape(groups, members, capacity, width)
    side_scales = got_scales.reshape(groups, members, capacity, block_count)
    side_gates = got_gates.reshape(groups, members, capacity, GROUP_EXP)
    pair_values, pair_scales, pair_slot_gates = (
        lax.all_gather(side_values[None], "rep", axis=0, tiled=True),
        lax.all_gather(side_scales[None], "rep", axis=0, tiled=True),
        lax.all_gather(side_gates[None], "rep", axis=0, tiled=True),
    )
    arrived = dequantize(pair_values, pair_scales).reshape(-1, width)
    gate_part = jnp.dot(arrived, gate_local, preferred_element_type=jnp.float32)
    up_part = jnp.dot(arrived, up_local, preferred_element_type=jnp.float32)
    hidden = (jax.nn.silu(gate_part) * up_part).astype(jnp.bfloat16)
    summed = jnp.dot(
        lax.all_gather(hidden, "expert", axis=1, tiled=True),
        down_local,
        preferred_element_type=jnp.float32,
    )
    expert_out = summed.astype(jnp.bfloat16)
    own_side = (jnp.arange(GROUP_EXP, dtype=jnp.int32) == lax.axis_index("rep")).astype(jnp.float32)
    gate_mine = jnp.sum(
        pair_slot_gates.reshape(-1, GROUP_EXP).astype(jnp.float32) * own_side[None, :], axis=1
    )
    gated_out = (gate_mine[:, None] * expert_out.astype(jnp.float32)).reshape(
        GROUP_EXP, -1, column_count
    )
    group_sum = lax.psum_scatter(
        gated_out.astype(jnp.bfloat16), "rep", scatter_dimension=0, tiled=True
    )
    outputs = group_sum.reshape(groups, members, capacity, column_count)
    flat_back = lax.all_to_all(
        outputs.reshape(groups * members, capacity, column_count),
        ("node", "expert"),
        split_axis=0,
        concat_axis=0,
        tiled=True,
    )
    returned = flat_back.reshape(groups, members, capacity, column_count)
    return_table = jnp.transpose(returned, (0, 2, 1, 3)).reshape(
        groups * capacity, members * column_count
    )
    combined = jnp.dot(assign.T, return_table, preferred_element_type=jnp.float32)
    return combined.astype(jnp.bfloat16)


NODES = 4
SLOTS = 8
USED = 6
BLOCKS = 3
MESH = pl.DeviceIdType.MESH


def by_slots(value):
    return value.reshape(value.shape[0] // SLOTS, SLOTS, value.shape[1])


def pack(value):
    wide = value.shape[1] // 4
    spare = by_slots(value[:, 3 * wide:])
    row = lax.broadcasted_iota(jnp.int32, spare.shape, 1)
    blocks = []
    for b in range(BLOCKS):
        moved = pltpu.roll(spare, USED - 2 * b, 1)
        kept = by_slots(value[:, b * wide:(b + 1) * wide])
        blocks.append(jnp.where(row >= USED, moved, kept).reshape(value.shape[0], wide))
    return blocks


def unpack_spare(blocks):
    threes = [by_slots(block) for block in blocks]
    row = lax.broadcasted_iota(jnp.int32, threes[0].shape, 1)
    moved = [pltpu.roll(threes[b], SLOTS - USED + 2 * b, 1) for b in range(BLOCKS)]
    spare = jnp.where(row < 2, moved[0], jnp.where(row < 4, moved[1], moved[2]))
    return spare.reshape(blocks[0].shape)


def fused_kernel(
    tok_hbm, scale_hbm, ids_hbm, gate_hbm, gate_w_hbm, up_hbm, down_hbm, out_ref,
    tok_ref, scale_ref, ids_ref, gate_ref,
    wg, wu, wd, zout, slabs, rows, gates, acc_g, acc_u, hid_out, hid_in, hidden, acc_d,
    mate_out, mate_in, sums, back_out, back_in, final, last_out, last_in, place, place_in,
    w_sem, recv_sem, z_sem, x_sem, m_sem, h_sem, r_sem, b_send, b_recv, f_sem, p_sem,
):
    part = lax.axis_index("parts")
    n = lax.axis_index("node")
    e = lax.axis_index("expert")
    r = lax.axis_index("rep")
    width = tok_ref.shape[1]
    half = width // 2
    ff = wg.shape[1]
    step = half // 4
    packed = BLOCKS * step
    bf16, f32 = jnp.bfloat16, jnp.float32

    small = [
        pltpu.make_async_copy(src, dst, w_sem.at[3 + i])
        for i, (src, dst) in enumerate(
            [(tok_hbm, tok_ref), (scale_hbm, scale_ref), (ids_hbm, ids_ref), (gate_hbm, gate_ref)]
        )
    ]
    weights = [
        pltpu.make_async_copy(gate_w_hbm.at[0], wg, w_sem.at[0]),
        pltpu.make_async_copy(up_hbm.at[0], wu, w_sem.at[1]),
        pltpu.make_async_copy(down_hbm.at[0], wd, w_sem.at[2]),
    ]
    for copy in small + weights:
        copy.start()

    near = n + 1 - 2 * (n % 2)
    peers = [(n + 2) % 4, 3 - n, near]
    z_devs = [(part, p, e, r) for p in peers]
    x_dev = (part, n, 1 - e, r)
    m_dev = (part, n, e, 1 - r)

    barrier = pltpu.get_barrier_semaphore()
    for dev in z_devs + [x_dev, m_dev]:
        pl.semaphore_signal(barrier, inc=1, device_id=dev, device_id_type=MESH)

    def slot(a, b, c):
        return (a * 2 + b) * 2 + c

    me = slot(n, e, r)
    for copy in small:
        copy.wait()
    lane = lax.broadcasted_iota(jnp.int32, (SLOTS, 128), 1)
    table = jnp.zeros(lane.shape, f32)
    hit = jnp.zeros(lane.shape, f32)
    row = lax.broadcasted_iota(jnp.int32, lane.shape, 0)
    eye = jnp.where(row == lane, 1.0, 0.0)[:, :SLOTS].astype(bf16)
    turn = (((1,), (1,)), ((), ()))
    ids_t = lax.dot_general(eye, ids_ref[...].astype(f32).astype(bf16), turn, preferred_element_type=f32)
    gate_t = lax.dot_general(eye, gate_ref[...], turn, preferred_element_type=f32)
    lane_f = lane.astype(f32)
    first_f = ((lane >> 3) * 2).astype(f32)
    for k in range(ids_ref.shape[0]):
        chosen = ids_t[:, k:k + 1]
        table = table + jnp.where(chosen == lane_f, gate_t[:, k:k + 1], 0.0)
        hit = jnp.maximum(hit, jnp.where((chosen == first_f) | (chosen == first_f + 1.0), 1.0, 0.0))
    ahead = jnp.zeros(lane.shape, f32)
    for k in range(1, SLOTS):
        ahead = ahead + jnp.where(row >= k, pltpu.roll(hit, k, 0), 0.0)
    place[...] = jnp.where(ahead == (lane & 7).astype(f32), hit, 0.0)
    assign = place[...].T[:NODES * SLOTS].astype(bf16)
    scales = scale_ref[...].astype(f32)
    count = half // 128
    for h in range(2):
        pieces = [
            tok_ref[:, j * 128:(j + 1) * 128].astype(f32) * scales[:, j:j + 1]
            for j in range(h * count, (h + 1) * count)
        ]
        values = jnp.concatenate(pieces, axis=1).astype(bf16)
        placed = jnp.dot(assign, values, preferred_element_type=f32)
        for b, block in enumerate(pack(placed)):
            rows[h * 32:(h + 1) * 32, b * step:(b + 1) * step] = block.astype(bf16)
    slot_gates = jnp.dot(assign, table.astype(bf16), preferred_element_type=f32)
    for g in range(NODES):
        at = g * SLOTS
        for b in range(BLOCKS):
            span = slice(b * step, (b + 1) * step)
            lo = rows[0:32, span].astype(f32)[at:at + SLOTS]
            hi = rows[32:64, span].astype(f32)[at:at + SLOTS]
            zout[g, :, span] = jnp.concatenate([lo, hi], axis=0).astype(bf16)
        some = slot_gates[at:at + SLOTS]
        zout[g, :, packed:packed + 128] = jnp.concatenate([some, some], axis=0).astype(bf16)

    pl.semaphore_wait(barrier, 5)

    def cols(c):
        return pl.ds(c * step, step + (128 if c == BLOCKS - 1 else 0))

    def send(src_ref, src, c, sem, dev):
        copy = pltpu.make_async_remote_copy(
            src_ref=src_ref.at[:, cols(c)], dst_ref=slabs.at[src, :, cols(c)],
            send_sem=sem, recv_sem=recv_sem.at[src, c], device_id=dev, device_id_type=MESH,
        )
        copy.start()
        return copy

    def arrive(src, c):
        block = slabs.at[src, :, cols(c)]
        pltpu.make_async_remote_copy(
            src_ref=block, dst_ref=block, send_sem=m_sem.at[0, 0], recv_sem=recv_sem.at[src, c],
            device_id=m_dev, device_id_type=MESH,
        ).wait_recv()

    p_copy = pltpu.make_async_remote_copy(
        src_ref=place, dst_ref=place_in, send_sem=p_sem.at[0], recv_sem=p_sem.at[1],
        device_id=x_dev, device_id_type=MESH,
    )
    sent = []
    z_sent = []

    def issue(c):
        z_sent.append(
            [send(zout.at[peers[i]], me, c, z_sem.at[i, c], z_devs[i]) for i in range(3)]
        )
        sent.append(send(zout.at[n], me, c, x_sem.at[3, c], x_dev))
        sent.append(send(zout.at[n], me, c, m_sem.at[3, c], m_dev))

    def drained(c):
        for copy in z_sent[c]:
            copy.wait_send()

    issue(0)
    slabs[me] = zout[n]

    def pass_z(c):
        for i in range(3):
            src = slot(peers[i], e, r)
            arrive(src, c)
            sent.append(send(slabs.at[src], src, c, x_sem.at[i, c], x_dev))
            sent.append(send(slabs.at[src], src, c, m_sem.at[i, c], m_dev))

    def pass_x(c):
        for i, p in enumerate([n] + peers):
            src = slot(p, 1 - e, r)
            arrive(src, c)
            sent.append(send(slabs.at[src], src, c, m_sem.at[4 + i, c], m_dev))

    pairs = [(rr * NODES + nn, slot(nn, 0, rr), slot(nn, 1, rr)) for rr in range(2) for nn in range(NODES)]
    acc_g[...] = jnp.zeros_like(acc_g)
    acc_u[...] = jnp.zeros_like(acc_u)

    def project(first):
        span = slice(first, first + step)
        acc_g[...] += jnp.dot(rows[:, span], wg[span, :], preferred_element_type=f32)
        acc_u[...] += jnp.dot(rows[:, span], wu[span, :], preferred_element_type=f32)

    drained(0)
    issue(1)
    pass_z(0)
    drained(1)
    issue(2)
    p_copy.start()
    pass_z(1)
    for c in range(BLOCKS):
        if c == 1:
            pass_z(2)
        pass_x(c)
        for p in [n] + peers:
            arrive(slot(p, e, 1 - r), c)
            arrive(slot(p, 1 - e, 1 - r), c)
        span = slice(c * step, (c + 1) * step)
        for at, one, two in pairs:
            left = slabs[one, :, span].astype(f32)
            right = slabs[two, :, span].astype(f32)
            for h in range(2):
                cut = slice(h * SLOTS, (h + 1) * SLOTS)
                rows[at * 16:at * 16 + 16, h * half + c * step:h * half + (c + 1) * step] = (
                    jnp.concatenate([left[cut], right[cut]], axis=0).astype(bf16)
                )
        if c == 0:
            weights[0].wait()
            weights[1].wait()
        for h in range(2):
            project(h * half + c * step)
    for h in range(2):
        base = h * half
        for at in range(8):
            blocks = [
                rows[at * 16:at * 16 + 16, base + b * step:base + (b + 1) * step].astype(f32)
                for b in range(BLOCKS)
            ]
            rows[at * 16:at * 16 + 16, base + packed:base + half] = unpack_spare(blocks).astype(bf16)
        project(base + packed)

    drained(2)
    gate_v = acc_g[...]
    active = (gate_v / (1.0 + jnp.exp(-gate_v))) * acc_u[...]
    piece = ff // 4
    for b, block in enumerate(pack(active)):
        hid_out[:, b * piece:(b + 1) * piece] = block.astype(bf16)
    h_copy = pltpu.make_async_remote_copy(
        src_ref=hid_out, dst_ref=hid_in, send_sem=h_sem.at[0], recv_sem=h_sem.at[1],
        device_id=x_dev, device_id_type=MESH,
    )
    h_copy.start()
    hidden[...] = active.astype(bf16)

    mine = lax.broadcasted_iota(jnp.int32, (16, 128), 1) == n * 2 + r
    for at, one, two in pairs:
        left = slabs[one, :, packed:packed + 128].astype(f32)
        right = slabs[two, :, packed:packed + 128].astype(f32)
        both = jnp.concatenate([left[:SLOTS], right[:SLOTS]], axis=0)
        picked = jnp.sum(jnp.where(mine, both, 0.0), axis=1, keepdims=True)
        gates[at * 16:at * 16 + 16, :] = jnp.broadcast_to(picked, (16, 128))

    weights[2].wait()
    tiles = [slice(t * step, (t + 1) * step) for t in (3, 0, 1, 2)]
    own_ff = pl.ds(pl.multiple_of(e * ff, ff), ff)
    other_ff = pl.ds(pl.multiple_of((1 - e) * ff, ff), ff)
    for span in tiles:
        acc_d[:, span] = jnp.dot(hidden[...], wd[own_ff, span], preferred_element_type=f32)
    h_copy.wait()
    blocks = [hid_in[:, b * piece:(b + 1) * piece].astype(f32) for b in range(BLOCKS)]
    hidden[:, :BLOCKS * piece] = hid_in[...]
    hidden[:, BLOCKS * piece:] = unpack_spare(blocks).astype(bf16)
    group_rows = NODES * 16
    own_rows = pl.ds(pl.multiple_of(r * group_rows, group_rows), group_rows)
    mate_rows = pl.ds(pl.multiple_of((1 - r) * group_rows, group_rows), group_rows)
    r_copies = []
    b_copies = []

    def give(t):
        span = tiles[t]
        acc_d[:, span] += jnp.dot(hidden[...], wd[other_ff, span], preferred_element_type=f32)
        done = acc_d[mate_rows, span].astype(bf16).astype(f32)
        mate_out[:, span] = (done * gates[mate_rows, 0:1]).astype(bf16)
        copy = pltpu.make_async_remote_copy(
            src_ref=mate_out.at[:, span], dst_ref=mate_in.at[:, span],
            send_sem=r_sem.at[0, t], recv_sem=r_sem.at[1, t], device_id=m_dev, device_id_type=MESH,
        )
        copy.start()
        r_copies.append(copy)

    def take(t):
        span = tiles[t]
        r_copies[t].wait()
        done = acc_d[own_rows, span].astype(bf16).astype(f32)
        total = done * gates[own_rows, 0:1] + mate_in[:, span].astype(f32)
        if t == 0:
            sums[...] = total
            return
        b = t - 1
        spare = pltpu.roll(by_slots(sums[...]), USED - 2 * b, 1)
        slots = lax.broadcasted_iota(jnp.int32, spare.shape, 1)
        mixed = jnp.where(slots >= USED, spare, by_slots(total)).reshape(total.shape)
        back_out[:, span] = mixed.astype(bf16)
        for i in range(3):
            from_rows = pl.ds(pl.multiple_of(peers[i] * 16, 16), 16)
            copy = pltpu.make_async_remote_copy(
                src_ref=back_out.at[from_rows, span], dst_ref=back_in.at[n, :, span],
                send_sem=b_send.at[i, b], recv_sem=b_recv.at[n, b],
                device_id=z_devs[i], device_id_type=MESH,
            )
            copy.start()
            b_copies.append(copy)

    give(0)
    give(1)
    take(0)
    give(2)
    take(1)
    give(3)
    take(2)
    take(3)
    back_in[n] = back_out[pl.ds(pl.multiple_of(n * 16, 16), 16), :]
    p_copy.wait()
    own_lanes = place[...].astype(bf16)[:, :NODES * SLOTS]
    other_lanes = place_in[...].astype(bf16)[:, :NODES * SLOTS]
    f_copies = []

    def finish(b):
        span = slice(b * step, (b + 1) * step)
        theirs = jnp.dot(other_lanes, final[1 - e, :, span].astype(bf16), preferred_element_type=f32)
        last_out[:, span] = theirs
        copy = pltpu.make_async_remote_copy(
            src_ref=last_out.at[:, span], dst_ref=last_in.at[:, span],
            send_sem=f_sem.at[0, b], recv_sem=f_sem.at[1, b], device_id=x_dev, device_id_type=MESH,
        )
        copy.start()
        f_copies.append(copy)
        ours = jnp.dot(own_lanes, final[e, :, span].astype(bf16), preferred_element_type=f32)
        at = pl.multiple_of(e * half + b * step, step)
        out_ref[:, pl.ds(at, step)] = ours.astype(bf16)

    for b in range(BLOCKS):
        span = slice(b * step, (b + 1) * step)
        for i in range(3):
            block = back_in.at[peers[i], :, span]
            pltpu.make_async_remote_copy(
                src_ref=block, dst_ref=block,
                send_sem=b_send.at[i, b], recv_sem=b_recv.at[peers[i], b],
                device_id=z_devs[i], device_id_type=MESH,
            ).wait_recv()
        parts = [back_in[g, :, span].astype(f32) for g in range(NODES)]
        for h in range(2):
            final[h, :, span] = jnp.concatenate(
                [value[h * SLOTS:(h + 1) * SLOTS] for value in parts], axis=0
            )
        finish(b)
    for h in range(2):
        final[h, :, packed:] = unpack_spare(
            [final[h, :, b * step:(b + 1) * step] for b in range(BLOCKS)]
        )
    finish(BLOCKS)
    for b in range(BLOCKS + 1):
        f_copies[b].wait()
        at = pl.multiple_of((1 - e) * half + b * step, step)
        out_ref[:, pl.ds(at, step)] = last_in[:, b * step:(b + 1) * step].astype(bf16)
    for copy in sent + b_copies:
        copy.wait_send()


def fused_device(token_values, block_scales, expert_ids, gate_values, gate_proj, up_proj, down_proj):
    tok_rows, width = token_values.shape
    packed = width // 8 * BLOCKS
    ff = gate_proj.shape[2]
    total_rows = NODES * 4 * tok_rows
    column_count = down_proj.shape[2]
    vmem = pl.BlockSpec(memory_space=pltpu.VMEM)
    hbm = pl.BlockSpec(memory_space=pl.ANY)
    bf16, f32 = jnp.bfloat16, jnp.float32
    dma = pltpu.SemaphoreType.DMA
    return pl.pallas_call(
        fused_kernel,
        out_shape=jax.ShapeDtypeStruct((tok_rows, width), bf16),
        in_specs=[hbm] * 7,
        out_specs=vmem,
        scratch_shapes=[
            pltpu.VMEM(token_values.shape, bf16),
            pltpu.VMEM(block_scales.shape, bf16),
            pltpu.VMEM(expert_ids.shape[::-1], jnp.int32),
            pltpu.VMEM(gate_values.shape[::-1], bf16),
            pltpu.VMEM((width, ff), bf16),
            pltpu.VMEM((width, ff), bf16),
            pltpu.VMEM((2 * ff, column_count), bf16),
            pltpu.VMEM((NODES, 16, packed + 128), bf16),
            pltpu.VMEM((NODES * 4, 16, packed + 128), bf16),
            pltpu.VMEM((total_rows, width), bf16),
            pltpu.VMEM((total_rows, 128), f32),
            pltpu.VMEM((total_rows, ff), f32),
            pltpu.VMEM((total_rows, ff), f32),
            pltpu.VMEM((total_rows, ff // 4 * BLOCKS), bf16),
            pltpu.VMEM((total_rows, ff // 4 * BLOCKS), bf16),
            pltpu.VMEM((total_rows, ff), bf16),
            pltpu.VMEM((total_rows, column_count), f32),
            pltpu.VMEM((total_rows // 2, column_count), bf16),
            pltpu.VMEM((total_rows // 2, column_count), bf16),
            pltpu.VMEM((total_rows // 2, column_count // 4), f32),
            pltpu.VMEM((total_rows // 2, packed), bf16),
            pltpu.VMEM((NODES, 16, packed), bf16),
            pltpu.VMEM((2, NODES * SLOTS, column_count), f32),
            pltpu.VMEM((SLOTS, column_count), f32),
            pltpu.VMEM((SLOTS, column_count), f32),
            pltpu.VMEM((SLOTS, 128), f32),
            pltpu.VMEM((SLOTS, 128), f32),
            dma((7,)),
            dma((NODES * 4, BLOCKS)),
            dma((3, BLOCKS)),
            dma((4, BLOCKS)),
            dma((8, BLOCKS)),
            dma((2,)),
            dma((2, 4)),
            dma((3, BLOCKS)),
            dma((NODES, BLOCKS)),
            dma((2, BLOCKS + 1)),
            dma((2,)),
        ],
        compiler_params=pltpu.CompilerParams(
            collective_id=1, has_side_effects=True, vmem_limit_bytes=60 * 1024 * 1024
        ),
        cost_estimate=pl.CostEstimate(
            flops=2 * total_rows * width * ff * 3, bytes_accessed=6 * width * ff, transcendentals=0
        ),
    )(token_values, block_scales, expert_ids.T, gate_values.T, gate_proj, up_proj, down_proj)


def solution(mesh):
    sizes = mesh.shape
    fits = (sizes["node"], sizes["expert"], sizes["rep"]) == (4, 2, 2)
    return jax.shard_map(
        fused_device if fits else per_device,
        mesh=mesh,
        in_specs=(
            P(("parts", "node", "expert", "rep"), None),
            P(("parts", "node", "expert", "rep"), None),
            P(("parts", "node", "expert", "rep"), None),
            P(("parts", "node", "expert", "rep"), None),
            P(("node", "rep"), None, "expert"),
            P(("node", "rep"), None, "expert"),
            P(("node", "rep"), None, "expert"),
        ),
        out_specs=P(("parts", "node", "expert", "rep"), None),
        check_vma=False,
    )
```

```python
import functools

import jax
import jax.numpy as jnp
from jax import lax
from jax.experimental import pallas as pl
from jax.experimental.pallas import tpu as pltpu
from jax.sharding import PartitionSpec as P

LIMIT = 3
GROUP_EXP = 2


def dequantize(values, scales):
    lead_dims = values.shape[:-1]
    width = values.shape[-1]
    blocks = (
        values.astype(jnp.float32).reshape(lead_dims + (width // 128, 128))
        * scales.astype(jnp.float32)[..., None]
    )
    return blocks.reshape(values.shape).astype(jnp.bfloat16)


def per_device(token_values, block_scales, expert_ids, gate_values, gate_proj, up_proj, down_proj):
    groups = lax.axis_size("node")
    members = lax.axis_size("expert")
    tok_rows, width = token_values.shape
    block_count = block_scales.shape[1]
    capacity = (LIMIT * tok_rows + groups - 1) // groups
    gate_local = gate_proj[0]
    up_local = up_proj[0]
    down_local = down_proj[0]
    column_count = down_local.shape[1]
    group_index = expert_ids // GROUP_EXP
    side_index = expert_ids % GROUP_EXP
    group_hit = group_index[:, :, None] == jnp.arange(groups, dtype=jnp.int32)[None, None, :]
    in_group = jnp.any(group_hit, axis=1).astype(jnp.int32)
    ahead_count = jnp.cumsum(in_group, axis=0) - in_group
    slot_hit = (ahead_count[:, :, None] == jnp.arange(capacity, dtype=jnp.int32)[None, None, :]) & (
        in_group[:, :, None] > 0
    )
    assign = (
        jnp.transpose(slot_hit, (1, 2, 0)).reshape(groups * capacity, tok_rows).astype(jnp.bfloat16)
    )
    side_hit = (
        side_index[:, :, None] == jnp.arange(GROUP_EXP, dtype=jnp.int32)[None, None, :]
    ).astype(jnp.float32)
    pair_gates = jnp.einsum(
        "tkg,tks->tgs",
        group_hit.astype(jnp.float32),
        side_hit * gate_values.astype(jnp.float32)[:, :, None],
        precision=lax.Precision.HIGHEST,
    )
    send_gates = jnp.einsum(
        "tgc,tgs->gcs", slot_hit.astype(jnp.float32), pair_gates, precision=lax.Precision.HIGHEST
    ).astype(jnp.bfloat16)
    send_values = (
        jnp.dot(assign, token_values, preferred_element_type=jnp.float32)
        .astype(jnp.bfloat16)
        .reshape(groups, capacity, width)
    )
    send_scales = (
        jnp.dot(assign, block_scales, preferred_element_type=jnp.float32)
        .astype(jnp.bfloat16)
        .reshape(groups, capacity, block_count)
    )
    spread_values = jnp.broadcast_to(
        send_values[:, None], (groups, members, capacity, width)
    ).reshape(groups * members, capacity, width)
    spread_scales = jnp.broadcast_to(
        send_scales[:, None], (groups, members, capacity, block_count)
    ).reshape(groups * members, capacity, block_count)
    spread_gates = jnp.broadcast_to(
        send_gates[:, None], (groups, members, capacity, GROUP_EXP)
    ).reshape(groups * members, capacity, GROUP_EXP)
    got_values, got_scales, got_gates = (
        lax.all_to_all(spread_values, ("node", "expert"), split_axis=0, concat_axis=0, tiled=True),
        lax.all_to_all(spread_scales, ("node", "expert"), split_axis=0, concat_axis=0, tiled=True),
        lax.all_to_all(spread_gates, ("node", "expert"), split_axis=0, concat_axis=0, tiled=True),
    )
    side_values = got_values.reshape(groups, members, capacity, width)
    side_scales = got_scales.reshape(groups, members, capacity, block_count)
    side_gates = got_gates.reshape(groups, members, capacity, GROUP_EXP)
    pair_values, pair_scales, pair_slot_gates = (
        lax.all_gather(side_values[None], "rep", axis=0, tiled=True),
        lax.all_gather(side_scales[None], "rep", axis=0, tiled=True),
        lax.all_gather(side_gates[None], "rep", axis=0, tiled=True),
    )
    arrived = dequantize(pair_values, pair_scales).reshape(-1, width)
    gate_part = jnp.dot(arrived, gate_local, preferred_element_type=jnp.float32)
    up_part = jnp.dot(arrived, up_local, preferred_element_type=jnp.float32)
    hidden = (jax.nn.silu(gate_part) * up_part).astype(jnp.bfloat16)
    summed = jnp.dot(
        lax.all_gather(hidden, "expert", axis=1, tiled=True),
        down_local,
        preferred_element_type=jnp.float32,
    )
    expert_out = summed.astype(jnp.bfloat16)
    own_side = (jnp.arange(GROUP_EXP, dtype=jnp.int32) == lax.axis_index("rep")).astype(jnp.float32)
    gate_mine = jnp.sum(
        pair_slot_gates.reshape(-1, GROUP_EXP).astype(jnp.float32) * own_side[None, :], axis=1
    )
    gated_out = (gate_mine[:, None] * expert_out.astype(jnp.float32)).reshape(
        GROUP_EXP, -1, column_count
    )
    group_sum = lax.psum_scatter(
        gated_out.astype(jnp.bfloat16), "rep", scatter_dimension=0, tiled=True
    )
    outputs = group_sum.reshape(groups, members, capacity, column_count)
    flat_back = lax.all_to_all(
        outputs.reshape(groups * members, capacity, column_count),
        ("node", "expert"),
        split_axis=0,
        concat_axis=0,
        tiled=True,
    )
    returned = flat_back.reshape(groups, members, capacity, column_count)
    return_table = jnp.transpose(returned, (0, 2, 1, 3)).reshape(
        groups * capacity, members * column_count
    )
    combined = jnp.dot(assign.T, return_table, preferred_element_type=jnp.float32)
    return combined.astype(jnp.bfloat16)


NODES = 4
SLOTS = 8
USED = 6
BLOCKS = 3
MESH = pl.DeviceIdType.MESH


def by_slots(value):
    return value.reshape(value.shape[0] // SLOTS, SLOTS, value.shape[1])


def pack(value):
    wide = value.shape[1] // 4
    spare = by_slots(value[:, 3 * wide:])
    row = lax.broadcasted_iota(jnp.int32, spare.shape, 1)
    blocks = []
    for b in range(BLOCKS):
        moved = pltpu.roll(spare, USED - 2 * b, 1)
        kept = by_slots(value[:, b * wide:(b + 1) * wide])
        blocks.append(jnp.where(row >= USED, moved, kept).reshape(value.shape[0], wide))
    return blocks


def unpack_spare(blocks):
    threes = [by_slots(block) for block in blocks]
    row = lax.broadcasted_iota(jnp.int32, threes[0].shape, 1)
    moved = [pltpu.roll(threes[b], SLOTS - USED + 2 * b, 1) for b in range(BLOCKS)]
    spare = jnp.where(row < 2, moved[0], jnp.where(row < 4, moved[1], moved[2]))
    return spare.reshape(blocks[0].shape)


def fused_kernel(
    tok_hbm, scale_hbm, ids_hbm, gate_hbm, gate_w_hbm, up_hbm, down_hbm, out_ref,
    tok_ref, scale_ref, ids_ref, gate_ref,
    wg, wu, wd, zout, slabs, rows, gates, acc_g, acc_u, hid_out, hid_in, hidden, acc_d,
    mate_out, mate_in, sums, back_out, back_in, final, last_out, last_in, place, place_in,
    w_sem, recv_sem, z_sem, x_sem, m_sem, h_sem, r_sem, b_send, b_recv, f_sem, p_sem,
):
    part = lax.axis_index("parts")
    n = lax.axis_index("node")
    e = lax.axis_index("expert")
    r = lax.axis_index("rep")
    width = tok_ref.shape[1]
    half = width // 2
    ff = wg.shape[1]
    step = half // 4
    packed = BLOCKS * step
    bf16, f32 = jnp.bfloat16, jnp.float32

    small = [
        pltpu.make_async_copy(src, dst, w_sem.at[3 + i])
        for i, (src, dst) in enumerate(
            [(tok_hbm, tok_ref), (scale_hbm, scale_ref), (ids_hbm, ids_ref), (gate_hbm, gate_ref)]
        )
    ]
    weights = [
        pltpu.make_async_copy(gate_w_hbm.at[0], wg, w_sem.at[0]),
        pltpu.make_async_copy(up_hbm.at[0], wu, w_sem.at[1]),
        pltpu.make_async_copy(down_hbm.at[0], wd, w_sem.at[2]),
    ]
    for copy in small + weights:
        copy.start()

    near = n + 1 - 2 * (n % 2)
    peers = [near, (n + 2) % 4, 3 - n]
    z_devs = [(part, p, e, r) for p in peers]
    x_dev = (part, n, 1 - e, r)
    m_dev = (part, n, e, 1 - r)

    barrier = pltpu.get_barrier_semaphore()
    for dev in z_devs + [x_dev, m_dev]:
        pl.semaphore_signal(barrier, inc=1, device_id=dev, device_id_type=MESH)

    def slot(a, b, c):
        return (a * 2 + b) * 2 + c

    me = slot(n, e, r)
    for copy in small:
        copy.wait()
    lane = lax.broadcasted_iota(jnp.int32, (SLOTS, 128), 1)
    table = jnp.zeros(lane.shape, f32)
    hit = jnp.zeros(lane.shape, f32)
    row = lax.broadcasted_iota(jnp.int32, lane.shape, 0)
    eye = jnp.where(row == lane, 1.0, 0.0)[:, :SLOTS].astype(bf16)
    turn = (((1,), (1,)), ((), ()))
    ids_t = lax.dot_general(eye, ids_ref[...].astype(f32).astype(bf16), turn, preferred_element_type=f32)
    gate_t = lax.dot_general(eye, gate_ref[...], turn, preferred_element_type=f32)
    lane_f = lane.astype(f32)
    first_f = ((lane >> 3) * 2).astype(f32)
    for k in range(ids_ref.shape[0]):
        chosen = ids_t[:, k:k + 1]
        table = table + jnp.where(chosen == lane_f, gate_t[:, k:k + 1], 0.0)
        hit = jnp.maximum(hit, jnp.where((chosen == first_f) | (chosen == first_f + 1.0), 1.0, 0.0))
    ahead = jnp.zeros(lane.shape, f32)
    for k in range(1, SLOTS):
        ahead = ahead + jnp.where(row >= k, pltpu.roll(hit, k, 0), 0.0)
    place[...] = jnp.where(ahead == (lane & 7).astype(f32), hit, 0.0)
    assign = place[...].T[:NODES * SLOTS].astype(bf16)
    scales = scale_ref[...].astype(f32)
    count = half // 128
    for h in range(2):
        pieces = [
            tok_ref[:, j * 128:(j + 1) * 128].astype(f32) * scales[:, j:j + 1]
            for j in range(h * count, (h + 1) * count)
        ]
        values = jnp.concatenate(pieces, axis=1).astype(bf16)
        placed = jnp.dot(assign, values, preferred_element_type=f32)
        for b, block in enumerate(pack(placed)):
            rows[h * 32:(h + 1) * 32, b * step:(b + 1) * step] = block.astype(bf16)
    slot_gates = jnp.dot(assign, table.astype(bf16), preferred_element_type=f32)
    for g in range(NODES):
        at = g * SLOTS
        for b in range(BLOCKS):
            span = slice(b * step, (b + 1) * step)
            lo = rows[0:32, span].astype(f32)[at:at + SLOTS]
            hi = rows[32:64, span].astype(f32)[at:at + SLOTS]
            zout[g, :, span] = jnp.concatenate([lo, hi], axis=0).astype(bf16)
        some = slot_gates[at:at + SLOTS]
        zout[g, :, packed:packed + 128] = jnp.concatenate([some, some], axis=0).astype(bf16)

    pl.semaphore_wait(barrier, 5)

    def cols(c):
        return pl.ds(c * step, step + (128 if c == BLOCKS - 1 else 0))

    def send(src_ref, src, c, sem, dev):
        copy = pltpu.make_async_remote_copy(
            src_ref=src_ref.at[:, cols(c)], dst_ref=slabs.at[src, :, cols(c)],
            send_sem=sem, recv_sem=recv_sem.at[src, c], device_id=dev, device_id_type=MESH,
        )
        copy.start()
        return copy

    def arrive(src, c):
        block = slabs.at[src, :, cols(c)]
        pltpu.make_async_remote_copy(
            src_ref=block, dst_ref=block, send_sem=m_sem.at[0, 0], recv_sem=recv_sem.at[src, c],
            device_id=m_dev, device_id_type=MESH,
        ).wait_recv()

    p_copy = pltpu.make_async_remote_copy(
        src_ref=place, dst_ref=place_in, send_sem=p_sem.at[0], recv_sem=p_sem.at[1],
        device_id=x_dev, device_id_type=MESH,
    )
    sent = []
    z_sent = []

    def issue(c):
        z_sent.append(
            [send(zout.at[peers[i]], me, c, z_sem.at[i, c], z_devs[i]) for i in range(3)]
        )
        sent.append(send(zout.at[n], me, c, x_sem.at[3, c], x_dev))
        sent.append(send(zout.at[n], me, c, m_sem.at[3, c], m_dev))

    def drained(c):
        for copy in z_sent[c]:
            copy.wait_send()

    issue(0)
    slabs[me] = zout[n]

    def pass_z(c):
        for i in range(3):
            src = slot(peers[i], e, r)
            arrive(src, c)
            sent.append(send(slabs.at[src], src, c, x_sem.at[i, c], x_dev))
            sent.append(send(slabs.at[src], src, c, m_sem.at[i, c], m_dev))

    def pass_x(c):
        for i, p in enumerate([n] + peers):
            src = slot(p, 1 - e, r)
            arrive(src, c)
            sent.append(send(slabs.at[src], src, c, m_sem.at[4 + i, c], m_dev))

    pairs = [(rr * NODES + nn, slot(nn, 0, rr), slot(nn, 1, rr)) for rr in range(2) for nn in range(NODES)]
    acc_g[...] = jnp.zeros_like(acc_g)
    acc_u[...] = jnp.zeros_like(acc_u)

    def project(first):
        span = slice(first, first + step)
        acc_g[...] += jnp.dot(rows[:, span], wg[span, :], preferred_element_type=f32)
        acc_u[...] += jnp.dot(rows[:, span], wu[span, :], preferred_element_type=f32)

    issue(1)
    drained(0)
    issue(2)
    pass_z(0)
    drained(1)
    p_copy.start()
    pass_z(1)
    for c in range(BLOCKS):
        if c == 1:
            pass_z(2)
        pass_x(c)
        for p in [n] + peers:
            arrive(slot(p, e, 1 - r), c)
            arrive(slot(p, 1 - e, 1 - r), c)
        span = slice(c * step, (c + 1) * step)
        for at, one, two in pairs:
            left = slabs[one, :, span].astype(f32)
            right = slabs[two, :, span].astype(f32)
            for h in range(2):
                cut = slice(h * SLOTS, (h + 1) * SLOTS)
                rows[at * 16:at * 16 + 16, h * half + c * step:h * half + (c + 1) * step] = (
                    jnp.concatenate([left[cut], right[cut]], axis=0).astype(bf16)
                )
        if c == 0:
            weights[0].wait()
            weights[1].wait()
        for h in range(2):
            project(h * half + c * step)
    for h in range(2):
        base = h * half
        for at in range(8):
            blocks = [
                rows[at * 16:at * 16 + 16, base + b * step:base + (b + 1) * step].astype(f32)
                for b in range(BLOCKS)
            ]
            rows[at * 16:at * 16 + 16, base + packed:base + half] = unpack_spare(blocks).astype(bf16)
        project(base + packed)

    drained(2)
    gate_v = acc_g[...]
    active = (gate_v / (1.0 + jnp.exp(-gate_v))) * acc_u[...]
    piece = ff // 4
    for b, block in enumerate(pack(active)):
        hid_out[:, b * piece:(b + 1) * piece] = block.astype(bf16)
    h_copy = pltpu.make_async_remote_copy(
        src_ref=hid_out, dst_ref=hid_in, send_sem=h_sem.at[0], recv_sem=h_sem.at[1],
        device_id=x_dev, device_id_type=MESH,
    )
    h_copy.start()
    hidden[...] = active.astype(bf16)

    mine = lax.broadcasted_iota(jnp.int32, (16, 128), 1) == n * 2 + r
    for at, one, two in pairs:
        left = slabs[one, :, packed:packed + 128].astype(f32)
        right = slabs[two, :, packed:packed + 128].astype(f32)
        both = jnp.concatenate([left[:SLOTS], right[:SLOTS]], axis=0)
        picked = jnp.sum(jnp.where(mine, both, 0.0), axis=1, keepdims=True)
        gates[at * 16:at * 16 + 16, :] = jnp.broadcast_to(picked, (16, 128))

    weights[2].wait()
    tiles = [slice(t * step, (t + 1) * step) for t in (3, 0, 1, 2)]
    own_ff = pl.ds(pl.multiple_of(e * ff, ff), ff)
    other_ff = pl.ds(pl.multiple_of((1 - e) * ff, ff), ff)
    for span in tiles:
        acc_d[:, span] = jnp.dot(hidden[...], wd[own_ff, span], preferred_element_type=f32)
    h_copy.wait()
    blocks = [hid_in[:, b * piece:(b + 1) * piece].astype(f32) for b in range(BLOCKS)]
    hidden[:, :BLOCKS * piece] = hid_in[...]
    hidden[:, BLOCKS * piece:] = unpack_spare(blocks).astype(bf16)
    group_rows = NODES * 16
    own_rows = pl.ds(pl.multiple_of(r * group_rows, group_rows), group_rows)
    mate_rows = pl.ds(pl.multiple_of((1 - r) * group_rows, group_rows), group_rows)
    r_copies = []
    b_copies = []

    def give(t):
        span = tiles[t]
        acc_d[:, span] += jnp.dot(hidden[...], wd[other_ff, span], preferred_element_type=f32)
        done = acc_d[mate_rows, span].astype(bf16).astype(f32)
        mate_out[:, span] = (done * gates[mate_rows, 0:1]).astype(bf16)
        copy = pltpu.make_async_remote_copy(
            src_ref=mate_out.at[:, span], dst_ref=mate_in.at[:, span],
            send_sem=r_sem.at[0, t], recv_sem=r_sem.at[1, t], device_id=m_dev, device_id_type=MESH,
        )
        copy.start()
        r_copies.append(copy)

    def take(t):
        span = tiles[t]
        r_copies[t].wait()
        done = acc_d[own_rows, span].astype(bf16).astype(f32)
        total = done * gates[own_rows, 0:1] + mate_in[:, span].astype(f32)
        if t == 0:
            sums[...] = total
            return
        b = t - 1
        spare = pltpu.roll(by_slots(sums[...]), USED - 2 * b, 1)
        slots = lax.broadcasted_iota(jnp.int32, spare.shape, 1)
        mixed = jnp.where(slots >= USED, spare, by_slots(total)).reshape(total.shape)
        back_out[:, span] = mixed.astype(bf16)
        for i in range(3):
            from_rows = pl.ds(pl.multiple_of(peers[i] * 16, 16), 16)
            copy = pltpu.make_async_remote_copy(
                src_ref=back_out.at[from_rows, span], dst_ref=back_in.at[n, :, span],
                send_sem=b_send.at[i, b], recv_sem=b_recv.at[n, b],
                device_id=z_devs[i], device_id_type=MESH,
            )
            copy.start()
            b_copies.append(copy)

    give(0)
    give(1)
    take(0)
    give(2)
    take(1)
    give(3)
    take(2)
    take(3)
    back_in[n] = back_out[pl.ds(pl.multiple_of(n * 16, 16), 16), :]
    p_copy.wait()
    own_lanes = place[...].astype(bf16)[:, :NODES * SLOTS]
    other_lanes = place_in[...].astype(bf16)[:, :NODES * SLOTS]
    f_copies = []

    def finish(b):
        span = slice(b * step, (b + 1) * step)
        theirs = jnp.dot(other_lanes, final[1 - e, :, span].astype(bf16), preferred_element_type=f32)
        last_out[:, span] = theirs
        copy = pltpu.make_async_remote_copy(
            src_ref=last_out.at[:, span], dst_ref=last_in.at[:, span],
            send_sem=f_sem.at[0, b], recv_sem=f_sem.at[1, b], device_id=x_dev, device_id_type=MESH,
        )
        copy.start()
        f_copies.append(copy)
        ours = jnp.dot(own_lanes, final[e, :, span].astype(bf16), preferred_element_type=f32)
        at = pl.multiple_of(e * half + b * step, step)
        out_ref[:, pl.ds(at, step)] = ours.astype(bf16)

    for b in range(BLOCKS):
        span = slice(b * step, (b + 1) * step)
        for i in range(3):
            block = back_in.at[peers[i], :, span]
            pltpu.make_async_remote_copy(
                src_ref=block, dst_ref=block,
                send_sem=b_send.at[i, b], recv_sem=b_recv.at[peers[i], b],
                device_id=z_devs[i], device_id_type=MESH,
            ).wait_recv()
        parts = [back_in[g, :, span].astype(f32) for g in range(NODES)]
        for h in range(2):
            final[h, :, span] = jnp.concatenate(
                [value[h * SLOTS:(h + 1) * SLOTS] for value in parts], axis=0
            )
        finish(b)
    for h in range(2):
        final[h, :, packed:] = unpack_spare(
            [final[h, :, b * step:(b + 1) * step] for b in range(BLOCKS)]
        )
    finish(BLOCKS)
    for b in range(BLOCKS + 1):
        f_copies[b].wait()
        at = pl.multiple_of((1 - e) * half + b * step, step)
        out_ref[:, pl.ds(at, step)] = last_in[:, b * step:(b + 1) * step].astype(bf16)
    for copy in sent + b_copies:
        copy.wait_send()


def fused_device(token_values, block_scales, expert_ids, gate_values, gate_proj, up_proj, down_proj):
    tok_rows, width = token_values.shape
    packed = width // 8 * BLOCKS
    ff = gate_proj.shape[2]
    total_rows = NODES * 4 * tok_rows
    column_count = down_proj.shape[2]
    vmem = pl.BlockSpec(memory_space=pltpu.VMEM)
    hbm = pl.BlockSpec(memory_space=pl.ANY)
    bf16, f32 = jnp.bfloat16, jnp.float32
    dma = pltpu.SemaphoreType.DMA
    return pl.pallas_call(
        fused_kernel,
        out_shape=jax.ShapeDtypeStruct((tok_rows, width), bf16),
        in_specs=[hbm] * 7,
        out_specs=vmem,
        scratch_shapes=[
            pltpu.VMEM(token_values.shape, bf16),
            pltpu.VMEM(block_scales.shape, bf16),
            pltpu.VMEM(expert_ids.shape[::-1], jnp.int32),
            pltpu.VMEM(gate_values.shape[::-1], bf16),
            pltpu.VMEM((width, ff), bf16),
            pltpu.VMEM((width, ff), bf16),
            pltpu.VMEM((2 * ff, column_count), bf16),
            pltpu.VMEM((NODES, 16, packed + 128), bf16),
            pltpu.VMEM((NODES * 4, 16, packed + 128), bf16),
            pltpu.VMEM((total_rows, width), bf16),
            pltpu.VMEM((total_rows, 128), f32),
            pltpu.VMEM((total_rows, ff), f32),
            pltpu.VMEM((total_rows, ff), f32),
            pltpu.VMEM((total_rows, ff // 4 * BLOCKS), bf16),
            pltpu.VMEM((total_rows, ff // 4 * BLOCKS), bf16),
            pltpu.VMEM((total_rows, ff), bf16),
            pltpu.VMEM((total_rows, column_count), f32),
            pltpu.VMEM((total_rows // 2, column_count), bf16),
            pltpu.VMEM((total_rows // 2, column_count), bf16),
            pltpu.VMEM((total_rows // 2, column_count // 4), f32),
            pltpu.VMEM((total_rows // 2, packed), bf16),
            pltpu.VMEM((NODES, 16, packed), bf16),
            pltpu.VMEM((2, NODES * SLOTS, column_count), f32),
            pltpu.VMEM((SLOTS, column_count), f32),
            pltpu.VMEM((SLOTS, column_count), f32),
            pltpu.VMEM((SLOTS, 128), f32),
            pltpu.VMEM((SLOTS, 128), f32),
            dma((7,)),
            dma((NODES * 4, BLOCKS)),
            dma((3, BLOCKS)),
            dma((4, BLOCKS)),
            dma((8, BLOCKS)),
            dma((2,)),
            dma((2, 4)),
            dma((3, BLOCKS)),
            dma((NODES, BLOCKS)),
            dma((2, BLOCKS + 1)),
            dma((2,)),
        ],
        compiler_params=pltpu.CompilerParams(
            collective_id=1, has_side_effects=True, vmem_limit_bytes=60 * 1024 * 1024
        ),
        cost_estimate=pl.CostEstimate(
            flops=2 * total_rows * width * ff * 3, bytes_accessed=6 * width * ff, transcendentals=0
        ),
    )(token_values, block_scales, expert_ids.T, gate_values.T, gate_proj, up_proj, down_proj)


def solution(mesh):
    sizes = mesh.shape
    fits = (sizes["node"], sizes["expert"], sizes["rep"]) == (4, 2, 2)
    return jax.shard_map(
        fused_device if fits else per_device,
        mesh=mesh,
        in_specs=(
            P(("parts", "node", "expert", "rep"), None),
            P(("parts", "node", "expert", "rep"), None),
            P(("parts", "node", "expert", "rep"), None),
            P(("parts", "node", "expert", "rep"), None),
            P(("node", "rep"), None, "expert"),
            P(("node", "rep"), None, "expert"),
            P(("node", "rep"), None, "expert"),
        ),
        out_specs=P(("parts", "node", "expert", "rep"), None),
        check_vma=False,
    )
```
